32 devices in a mesh: traj: 4 (over y, core), grid: 8 (over z, x).
Axes of the slice: x: 2, y: 2, z: 4, core: 2. Of those that a mesh axis runs over, the one named last changes fastest.
Arguments:
- state: bfloat16 [16, 24, 640, 1280], P('traj', None, 'grid'), may hold values from -6 to 6
- counts: int32 [16], replicated, may hold values from 0 to 4, as said below
- slot_perm: int32 [16], replicated, may hold values from 0 to 15, each once
- legendre: bfloat16 [640, 2, 320, 320], P(('traj', 'grid')), may hold values from -0.3125 to 0.3125
- quad_weight: float32 [320], replicated, may hold values from 0.5 to 1.5
- diffusion: float32 [24], replicated, may hold values from 0.5 to 20
Outputs:
- smoothed: bfloat16 [16, 24, 640, 1280], P('traj', None, 'grid')
The draws below stay inside these ranges and needn't reach their ends.
Inputs may be any that keep to these rules, and one draw needn't show every extreme that they name: Offspring counts of the 16 trajectories; they sum to 16, at least one trajectory has 4 copies, and at least one has none. `slot_perm`: each of the 16 slots appears once.
All inputs are finite; a program needn't handle non-finite values.
Results may differ from the reference program's by a relative error of at most 0.0077.
Values may be sent and summed in bfloat16 or wider, within the bound.
No kernel may reach another device: no remote copies, remote signals or barrier semaphores. Data moves between devices by JAX's collectives and lax.ppermute only.
A program may use at most 256 MiB of HBM per device.

```python
import math
import jax
import jax.numpy as jnp
from jax import lax

NLAT = 640
NLON = 1280
NM = 640
HALF = 320
FL = 24
TRAJ = 16


def draw_counts(key, part):
    key_one, key_two = jax.random.split(key, 2)
    most_copies = TRAJ // 4
    others = TRAJ - 1
    relabel = jax.random.permutation(key_one, TRAJ).astype(jnp.int32)
    seat_order = jax.random.permutation(key_two, others * most_copies).astype(jnp.int32)
    rest_owner = 1 + seat_order[:TRAJ - most_copies] // most_copies
    owner_rank = jnp.concatenate([jnp.zeros((most_copies,), jnp.int32), rest_owner.astype(jnp.int32)])
    owners = jnp.take(relabel, owner_rank)
    members = jnp.arange(TRAJ, dtype=jnp.int32)
    return jnp.sum((owners[:, None] == members[None, :]).astype(jnp.int32), axis=0).astype(jnp.int32)


def shard_levels(own_key, dims, shards, smallest, high):
    gain = 1.0
    for dim, blocks in shards:
        heights = jax.random.uniform(jax.random.fold_in(jax.random.fold_in(own_key, 6), dim), (blocks,), jnp.float32, smallest / len(shards), high / len(shards))
        gain = gain * jnp.repeat(jnp.exp(heights), dims[dim] // blocks).reshape((-1,) + (1,) * (len(dims) - 1 - dim))
    return gain


def gaussian(key, dims, scale, bound, pieces=(), held_as=jnp.bfloat16):
    gain = shard_levels(key, dims, pieces, -0.22, 0.18) if pieces else 1.0
    drawn = jax.random.normal(key, dims, jnp.float32) * scale * gain
    return jnp.minimum(jnp.maximum(drawn, -bound), bound).astype(held_as)


def setup_inputs(seed: int = 0) -> dict:
    arg_keys = jax.random.split(jax.random.key(seed), 7)
    state = gaussian(arg_keys[0], (TRAJ, FL, NLAT, NLON), 1.0, 6.0, ((0, 4), (2, 8)))
    counts = draw_counts(jax.random.fold_in(arg_keys[6], 71), 0)
    slot_perm = jax.random.permutation(arg_keys[2], TRAJ).astype(jnp.int32)
    legendre = gaussian(arg_keys[3], (NM, 2, HALF, HALF), HALF ** -0.5, 0.3125, ((0, 32),))
    quad_weight = jnp.clip(jax.random.uniform(arg_keys[4], (HALF,), jnp.float32, 0.5, 1.5), 0.5, 1.5)
    diffusion = jnp.clip(jnp.exp(jax.random.uniform(arg_keys[5], (FL,), jnp.float32, math.log(0.5), math.log(20.0))), 0.5, 20.0)
    return {"state": state, "counts": counts, "slot_perm": slot_perm, "legendre": legendre, "quad_weight": quad_weight, "diffusion": diffusion}


def parent_slots(counts, slot_perm):
    member_count = counts.shape[0]
    position = jnp.arange(member_count, dtype=jnp.int32)
    copy_end = jnp.cumsum(counts).astype(jnp.int32)
    copy_parent = jnp.sum((copy_end[None, :] <= position[:, None]).astype(jnp.int32), axis=1).astype(jnp.int32)
    landing = (slot_perm[:, None] == position[None, :]).astype(jnp.int32)
    return jnp.sum(landing * copy_parent[:, None], axis=0).astype(jnp.int32)


def trig_pair(wave_order, lon_count):
    lon_points = jnp.arange(lon_count, dtype=jnp.int32)
    phase_angle = ((wave_order[:, None] * lon_points[None, :]) % lon_count).astype(jnp.float32) * (2.0 * math.pi / lon_count)
    return jnp.stack([jnp.cos(phase_angle), -jnp.sin(phase_angle)], axis=1)


def forward_table(wave_order, lon_count):
    return (trig_pair(wave_order, lon_count) / lon_count).astype(jnp.bfloat16)


def inverse_table(wave_order, lon_count):
    doubled = jnp.where(wave_order == 0, 1.0, 2.0).astype(jnp.float32)
    return (trig_pair(wave_order, lon_count) * doubled[:, None, None]).astype(jnp.bfloat16)


def spectral_filter(wave_rows, legendre_wide, wave_ids, quad_weight, diffusion):
    wave_here, halves, members, levels, lat_count = wave_rows.shape
    hemisphere = lat_count // 2
    north_rows = wave_rows[..., :hemisphere].astype(jnp.float32)
    south_rows = jnp.flip(wave_rows[..., hemisphere:], axis=-1).astype(jnp.float32)
    even_sum = ((north_rows + south_rows) * quad_weight).astype(jnp.bfloat16)
    odd_diff = ((north_rows - south_rows) * quad_weight).astype(jnp.bfloat16)
    paired = jnp.stack([even_sum, odd_diff], axis=1).reshape(wave_here, 2, halves * members * levels, hemisphere)
    spectrum = jnp.einsum("mpkl,mpcl->mpkc", legendre_wide, paired.astype(jnp.float32))
    parity = jnp.arange(2, dtype=jnp.int32)
    degree = 2 * jnp.arange(hemisphere, dtype=jnp.int32)[None, None, :] + (wave_ids[:, None, None] + parity[None, :, None]) % 2
    degree_ratio = (degree * (degree + 1)).astype(jnp.float32) / float(lat_count * (lat_count - 1))
    rate_cols = jnp.broadcast_to(diffusion, (halves, members, levels)).reshape(-1)
    damping = 1.0 / (1.0 + rate_cols[None, None, None, :] * (degree_ratio * degree_ratio)[..., None])
    retained = (degree >= wave_ids[:, None, None])[..., None]
    filtered = jnp.where(retained, spectrum * damping, 0.0).astype(jnp.bfloat16)
    returned = jnp.einsum("mpkl,mpkc->mpcl", legendre_wide, filtered.astype(jnp.float32))
    north_out = returned[:, 0] + returned[:, 1]
    south_out = returned[:, 0] - returned[:, 1]
    lat_rows = jnp.concatenate([north_out, jnp.flip(south_out, axis=-1)], axis=-1)
    return lat_rows.astype(jnp.bfloat16).reshape(wave_here, halves, members, levels, lat_count)


def reference(state, counts, slot_perm, legendre, quad_weight, diffusion):
    parents = parent_slots(counts, slot_perm)
    wave_ids = jnp.arange(NM, dtype=jnp.int32)
    forward_wide = forward_table(wave_ids, NLON).astype(jnp.float32)
    inverse_wide = inverse_table(wave_ids, NLON).astype(jnp.float32)
    legendre_wide = legendre.astype(jnp.float32)

    def one_member(parent):
        member = lax.dynamic_index_in_dim(state, parent, 0, keepdims=False).astype(jnp.float32)
        fourier = jnp.einsum("flj,mrj->mrfl", member, forward_wide).astype(jnp.bfloat16)
        waves_out = spectral_filter(fourier[:, :, None], legendre_wide, wave_ids, quad_weight, diffusion)
        smoothed = jnp.einsum("mrtfl,mrj->tflj", waves_out.astype(jnp.float32), inverse_wide)
        return smoothed[0].astype(jnp.bfloat16)

    return lax.map(one_member, parents)
```

```python
import math

import jax
import jax.numpy as jnp
import numpy as np
from jax import lax
from jax.sharding import PartitionSpec as P

FIELD_PARTS = 3
MOST_COPIES = 4


def parent_slots(counts, slot_perm):
    member_count = counts.shape[0]
    position = jnp.arange(member_count, dtype=jnp.int32)
    copy_end = jnp.cumsum(counts)
    copy_parent = jnp.sum((copy_end[None, :] <= position[:, None]).astype(jnp.int32), axis=1)
    landing = (slot_perm[:, None] == position[None, :]).astype(jnp.int32)
    return jnp.sum(landing * copy_parent[:, None], axis=0)


def survivor_lists(counts, slot_perm):
    member_count = counts.shape[0]
    position = jnp.arange(member_count, dtype=jnp.int32)
    alive = counts > 0
    rank = jnp.sum((position[None, :] < position[:, None]) & alive[None, :], axis=1).astype(jnp.int32)
    hit = alive[None, :] & (rank[None, :] == position[:, None])
    survivors = jnp.sum(hit * position[None, :], axis=1).astype(jnp.int32)
    parents = parent_slots(counts, slot_perm)
    slot_source = jnp.sum((parents[:, None] == position[None, :]) * rank[None, :], axis=1)
    return survivors, slot_source.astype(jnp.int32)


def trig_tables(lon_count):
    wave_count = lon_count // 2
    turn = np.arange(wave_count)[:, None] * np.arange(lon_count)[None, :] % lon_count
    phase = (turn.astype(np.float32) * np.float32(2.0 * math.pi / lon_count)).astype(np.float64)
    pair = np.stack([np.cos(phase), -np.sin(phase)], axis=1).astype(np.float32)
    doubled = np.where(np.arange(wave_count) == 0, 1.0, 2.0).astype(np.float32)
    forward = (pair / np.float32(lon_count)).astype(jnp.bfloat16)
    inverse = (pair * doubled[:, None, None]).astype(jnp.bfloat16)
    return forward.reshape(2 * wave_count, lon_count), inverse.reshape(2 * wave_count, lon_count)


def exchange(pieces, axis):
    size = lax.axis_size(axis)
    out = [pieces[0]]
    for s in range(1, size):
        out.append(lax.ppermute(pieces[s], axis, [(i, i ^ s) for i in range(size)]))
    return out


def whole_globe(legendre, quad_weight, slab_index, slab_count):
    wave_here, _, degree_count, hemisphere = legendre.shape
    mirror = np.eye(hemisphere, dtype=np.float32)[::-1].astype(jnp.bfloat16)
    weighted = (legendre.astype(jnp.float32) * quad_weight).astype(jnp.bfloat16)
    sign = jnp.array([1.0, -1.0], jnp.bfloat16)[None, :, None, None]

    def both(table):
        south = jnp.einsum("mpkl,lh->mpkh", table, mirror, preferred_element_type=jnp.float32)
        south = south.astype(jnp.bfloat16) * sign
        full = jnp.concatenate([table, south], axis=-1)
        full = full.reshape(wave_here, 2 * degree_count, slab_count, 2 * hemisphere // slab_count)
        order = slab_index ^ jnp.arange(slab_count, dtype=jnp.int32)
        full = jnp.take(full, order, axis=2)
        return full.reshape(wave_here, 2 * degree_count, 2 * hemisphere)

    return both(weighted), both(legendre)


def run(survivor_count, state, survivors, slot_source, legendre, quad_weight, diffusion):
    group_count = lax.axis_size("traj")
    slab_count = lax.axis_size("grid")
    group_index = lax.axis_index("traj")
    slab_index = lax.axis_index("grid")
    member_here, field_count, lat_here, lon_count = state.shape
    wave_count = lon_count // 2
    wave_here = wave_count // (group_count * slab_count)
    row_here = 2 * wave_here
    lat_count = lat_here * slab_count
    hemisphere = lat_count // 2
    field_here = field_count // FIELD_PARTS
    point_here = field_here * lat_here

    forward, inverse = trig_tables(lon_count)
    forward = jnp.asarray(forward)
    inverse = jnp.asarray(inverse).reshape(group_count, slab_count, row_here, lon_count)
    group_order = group_index ^ jnp.arange(group_count, dtype=jnp.int32)
    slab_order = slab_index ^ jnp.arange(slab_count, dtype=jnp.int32)
    inverse = jnp.take(jnp.take(inverse, group_order, axis=0), slab_order, axis=1)
    inverse = inverse.reshape(group_count * slab_count * row_here, lon_count)
    analysis, synthesis = whole_globe(legendre, quad_weight, slab_index, slab_count)

    wave_ids = (group_index * slab_count + slab_index) * wave_here + jnp.arange(
        wave_here, dtype=jnp.int32
    )
    parity = jnp.arange(2, dtype=jnp.int32)
    degree = (
        2 * jnp.arange(hemisphere, dtype=jnp.int32)[None, None, :]
        + (wave_ids[:, None, None] + parity[None, :, None]) % 2
    )
    degree_ratio = (degree * (degree + 1)).astype(jnp.float32) / float(lat_count * (lat_count - 1))
    ratio_square = (degree_ratio * degree_ratio).reshape(wave_here, 2 * hemisphere)
    retained = (degree >= wave_ids[:, None, None]).reshape(wave_here, 2 * hemisphere)

    survivor_at = (survivors // member_here ^ group_index) * member_here + survivors % member_here
    survivor_at = survivor_at[:survivor_count]
    slot_rows = slot_source.reshape(group_count, member_here)

    parts = []
    for part in range(FIELD_PARTS):
        block = state[:, part * field_here : (part + 1) * field_here].reshape(
            member_here, point_here, lon_count
        )
        fourier = jnp.einsum("wj,tcj->twc", forward, block, preferred_element_type=jnp.float32)
        fourier = fourier.astype(jnp.bfloat16).reshape(
            member_here, group_count, slab_count * row_here, point_here
        )
        pieces = [
            lax.dynamic_index_in_dim(fourier, group_index ^ s, 1, keepdims=False)
            for s in range(group_count)
        ]
        members = jnp.concatenate(exchange(pieces, "traj"), axis=0)
        kept = jnp.take(members, survivor_at, axis=0).reshape(
            survivor_count, slab_count, row_here, point_here
        )
        pieces = [
            lax.dynamic_index_in_dim(kept, slab_index ^ s, 1, keepdims=False)
            for s in range(slab_count)
        ]
        rows = jnp.stack(exchange(pieces, "grid"), axis=0)
        rows = rows.reshape(slab_count, survivor_count, wave_here, 2, field_here, lat_here)
        rows = rows.transpose(2, 1, 3, 4, 0, 5).reshape(wave_here, -1, lat_count)
        spectrum = jnp.einsum(
            "mql,mcl->mqc", analysis, rows, preferred_element_type=jnp.float32
        )
        rate = diffusion[part * field_here : (part + 1) * field_here]
        rate_cols = jnp.broadcast_to(rate, (survivor_count, 2, field_here)).reshape(-1)
        damping = 1.0 / (1.0 + rate_cols[None, None, :] * ratio_square[..., None])
        filtered = jnp.where(retained[..., None], spectrum * damping, 0.0).astype(jnp.bfloat16)
        waves = jnp.einsum(
            "mql,mqc->mcl", synthesis, filtered, preferred_element_type=jnp.float32
        ).astype(jnp.bfloat16)
        waves = waves.reshape(wave_here, survivor_count, 2, field_here, slab_count, lat_here)
        waves = waves.transpose(4, 1, 0, 2, 3, 5).reshape(
            slab_count, survivor_count, row_here, point_here
        )
        back = jnp.stack(exchange([waves[s] for s in range(slab_count)], "grid"), axis=1)
        pieces = [
            jnp.take(
                back, lax.dynamic_index_in_dim(slot_rows, group_index ^ s, 0, keepdims=False), axis=0
            )
            for s in range(group_count)
        ]
        slots = jnp.stack(exchange(pieces, "traj"), axis=1).reshape(
            member_here, -1, point_here
        )
        smoothed = jnp.einsum(
            "twc,wj->tcj", slots, inverse, preferred_element_type=jnp.float32
        )
        parts.append(
            smoothed.astype(jnp.bfloat16).reshape(member_here, field_here, lat_here, lon_count)
        )
    return jnp.concatenate(parts, axis=1)


def on_device(state, counts, slot_perm, legendre, quad_weight, diffusion):
    survivors, slot_source = survivor_lists(counts, slot_perm)
    most = counts.shape[0] - MOST_COPIES + 1
    return run(most, state, survivors, slot_source, legendre, quad_weight, diffusion)


def solution(mesh):
    return jax.shard_map(
        on_device,
        mesh=mesh,
        in_specs=(
            P("traj", None, "grid", None),
            P(),
            P(),
            P(("traj", "grid"), None, None, None),
            P(),
            P(),
        ),
        out_specs=P("traj", None, "grid", None),
        check_vma=False,
    )
```

```python
import math

import jax
import jax.numpy as jnp
import numpy as np
from jax import lax
from jax.experimental import pallas as pl
from jax.experimental.pallas import tpu as pltpu
from jax.sharding import PartitionSpec as P

FIELD_PARTS = 3
MOST_COPIES = 4
VMEM_BYTES = 60 * 2**20
NT = (((1,), (1,)), ((), ()))
TN = (((0,), (0,)), ((), ()))


def parent_slots(counts, slot_perm):
    member_count = counts.shape[0]
    position = jnp.arange(member_count, dtype=jnp.int32)
    copy_end = jnp.cumsum(counts)
    copy_parent = jnp.sum((copy_end[None, :] <= position[:, None]).astype(jnp.int32), axis=1)
    landing = (slot_perm[:, None] == position[None, :]).astype(jnp.int32)
    return jnp.sum(landing * copy_parent[:, None], axis=0)


def survivor_lists(counts, slot_perm):
    member_count = counts.shape[0]
    position = jnp.arange(member_count, dtype=jnp.int32)
    alive = counts > 0
    rank = jnp.sum((position[None, :] < position[:, None]) & alive[None, :], axis=1).astype(jnp.int32)
    hit = alive[None, :] & (rank[None, :] == position[:, None])
    survivors = jnp.sum(hit * position[None, :], axis=1).astype(jnp.int32)
    parents = parent_slots(counts, slot_perm)
    slot_source = jnp.sum((parents[:, None] == position[None, :]) * rank[None, :], axis=1)
    return survivors, slot_source.astype(jnp.int32)


def trig_tables(lon_count):
    wave_count = lon_count // 2
    turn = np.arange(wave_count)[:, None] * np.arange(lon_count)[None, :] % lon_count
    phase = (turn.astype(np.float32) * np.float32(2.0 * math.pi / lon_count)).astype(np.float64)
    pair = np.stack([np.cos(phase), -np.sin(phase)], axis=1).astype(np.float32)
    doubled = np.where(np.arange(wave_count) == 0, 1.0, 2.0).astype(np.float32)
    forward = (pair / np.float32(lon_count)).astype(jnp.bfloat16)
    inverse = (pair * doubled[:, None, None]).astype(jnp.bfloat16)
    return forward.reshape(2 * wave_count, lon_count), inverse.reshape(2 * wave_count, lon_count)


def exchange(pieces, axis):
    size = lax.axis_size(axis)
    out = [pieces[0]]
    for s in range(1, size):
        out.append(lax.ppermute(pieces[s], axis, [(i, i ^ s) for i in range(size)]))
    return out


def params():
    return pltpu.CompilerParams(vmem_limit_bytes=VMEM_BYTES)


def cost(flops, bytes_accessed):
    return pl.CostEstimate(flops=flops, bytes_accessed=bytes_accessed, transcendentals=0)


def dot(a, b, dims=(((1,), (0,)), ((), ()))):
    return lax.dot_general(a, b, dims, preferred_element_type=jnp.float32)


def analyse(table, state, part):
    group_count, rows, lon_count = table.shape
    member_here, _, points, _ = state.shape

    def kernel(table_ref, state_ref, *out_refs):
        block = state_ref[0, 0]
        for s in range(group_count):
            out_refs[s][0] = dot(table_ref[s], block, NT).astype(jnp.bfloat16)

    return pl.pallas_call(
        kernel,
        name="analyse",
        grid=(member_here,),
        in_specs=[
            pl.BlockSpec((group_count, rows, lon_count), lambda t: (0, 0, 0)),
            pl.BlockSpec((1, 1, points, lon_count), lambda t: (t, part, 0, 0)),
        ],
        out_specs=[pl.BlockSpec((1, rows, points), lambda t: (t, 0, 0))] * group_count,
        out_shape=[jax.ShapeDtypeStruct((member_here, rows, points), jnp.bfloat16)] * group_count,
        compiler_params=params(),
        cost_estimate=cost(
            2 * member_here * group_count * rows * lon_count * points,
            2 * member_here * points * (lon_count + group_count * rows),
        ),
    )(table, state)


def keep(place, survivors, sources, survivor_count):
    group_count = len(sources)
    member_here, slab_count, rows, points = sources[0].shape

    def kernel(place_ref, survivor_ref, *refs):
        source_refs = refs[:group_count]
        out_refs = refs[group_count : group_count + slab_count]
        sems = refs[-1]
        group, slab = place_ref[0], place_ref[1]
        for d in range(survivor_count):
            parent = survivor_ref[d]
            offset = lax.bitwise_xor(parent // member_here, group)
            member = parent % member_here
            for k in range(group_count):

                @pl.when(offset == k)
                def _(k=k, d=d, member=member):
                    for s in range(slab_count):
                        pltpu.make_async_copy(
                            source_refs[k].at[member, lax.bitwise_xor(slab, s)],
                            out_refs[s].at[d],
                            sems.at[s],
                        ).start()

        for s in range(slab_count):
            pltpu.make_async_copy(out_refs[s], out_refs[s], sems.at[s]).wait()

    return pl.pallas_call(
        kernel,
        name="keep",
        in_specs=[pl.BlockSpec(memory_space=pltpu.SMEM)] * 2
        + [pl.BlockSpec(memory_space=pl.ANY)] * group_count,
        out_specs=[pl.BlockSpec(memory_space=pl.ANY)] * slab_count,
        out_shape=[jax.ShapeDtypeStruct((survivor_count, rows, points), jnp.bfloat16)] * slab_count,
        scratch_shapes=[pltpu.SemaphoreType.DMA((slab_count,))],
        compiler_params=params(),
        cost_estimate=cost(0, 4 * survivor_count * slab_count * rows * points),
    )(place, survivors, *sources)


def spread(place, slot_source, sources, member_here, group_count):
    slab_count = len(sources)
    _, rows, points = sources[0].shape

    def kernel(place_ref, slot_ref, *refs):
        source_refs = refs[:slab_count]
        out_refs = refs[slab_count : slab_count + group_count]
        sems = refs[-1]
        group, slab = place_ref[0], place_ref[1]
        for k in range(group_count):
            for t in range(member_here):
                origin = slot_ref[lax.bitwise_xor(group, k) * member_here + t]
                for s in range(slab_count):
                    pltpu.make_async_copy(
                        source_refs[s].at[origin],
                        out_refs[k].at[t, lax.bitwise_xor(slab, s)],
                        sems.at[k],
                    ).start()
        for k in range(group_count):
            pltpu.make_async_copy(out_refs[k], out_refs[k], sems.at[k]).wait()

    return pl.pallas_call(
        kernel,
        name="spread",
        in_specs=[pl.BlockSpec(memory_space=pltpu.SMEM)] * 2
        + [pl.BlockSpec(memory_space=pl.ANY)] * slab_count,
        out_specs=[pl.BlockSpec(memory_space=pl.ANY)] * group_count,
        out_shape=[
            jax.ShapeDtypeStruct((member_here, slab_count, rows, points), jnp.bfloat16)
        ]
        * group_count,
        scratch_shapes=[pltpu.SemaphoreType.DMA((group_count,))],
        compiler_params=params(),
        cost_estimate=cost(0, 4 * group_count * member_here * slab_count * rows * points),
    )(place, slot_source, *sources)


def synthesise(place, table, sources, part, part_count, earlier):
    group_count, rows, lon_count = table.shape
    member_here, _, points = sources[0].shape

    def kernel(place_ref, table_ref, *refs):
        group = place_ref[0]
        total = dot(refs[0][0], table_ref[group], TN)
        for s in range(1, group_count):
            total += dot(refs[s][0], table_ref[lax.bitwise_xor(group, s)], TN)
        refs[-1][0, 0] = total.astype(jnp.bfloat16)

    given = [place, table, *sources]
    specs = [
        pl.BlockSpec(memory_space=pltpu.SMEM),
        pl.BlockSpec((group_count, rows, lon_count), lambda t: (0, 0, 0)),
    ] + [pl.BlockSpec((1, rows, points), lambda t: (t, 0, 0))] * group_count
    aliases = {}
    if earlier is not None:
        aliases = {len(given): 0}
        given.append(earlier)
        specs.append(pl.BlockSpec(memory_space=pl.ANY))
    return pl.pallas_call(
        kernel,
        name="synthesise",
        grid=(member_here,),
        in_specs=specs,
        out_specs=pl.BlockSpec((1, 1, points, lon_count), lambda t: (t, part, 0, 0)),
        out_shape=jax.ShapeDtypeStruct((member_here, part_count, points, lon_count), jnp.bfloat16),
        input_output_aliases=aliases,
        compiler_params=params(),
        cost_estimate=cost(
            2 * member_here * group_count * rows * lon_count * points,
            2 * member_here * points * (lon_count + group_count * rows),
        ),
    )(*given)


def spectral_filter(place, legendre, quad_weight, rates, sources, survivor_count, field_here):
    slab_count = len(sources)
    points = sources[0].shape[1]
    lat_here = points // field_here
    wave_here, _, degree_count, hemisphere = legendre.shape
    lat_count = 2 * hemisphere
    half_slabs = slab_count // 2
    row_here = 2 * wave_here
    used = 2 * survivor_count
    padded = -(-used // 16) * 16

    shuffle = np.zeros((wave_here, padded, survivor_count, wave_here, 2), np.float32)
    for m in range(wave_here):
        for d in range(survivor_count):
            for r in range(2):
                shuffle[m, 2 * d + r, d, m, r] = 1.0
    shuffle = shuffle.reshape(wave_here * padded, survivor_count * row_here)
    gather = jnp.asarray(shuffle.astype(jnp.bfloat16))
    scatter = jnp.asarray(shuffle.T.astype(jnp.bfloat16))
    mirror = jnp.asarray(np.eye(hemisphere, dtype=np.float32)[::-1].astype(jnp.bfloat16))

    def kernel(place_ref, gather_ref, scatter_ref, mirror_ref, weight_ref, rate_ref, table_ref, *refs):
        source_refs = refs[:slab_count]
        out_refs = refs[slab_count : 2 * slab_count]
        held, north_rows, south_rows = refs[2 * slab_count :]
        m = pl.program_id(0)
        group, slab = place_ref[0], place_ref[1]

        @pl.when(m == 0)
        def _():
            for s in range(slab_count):
                held[s] = dot(gather_ref[...], source_refs[s][...]).astype(jnp.bfloat16)

        here = pl.ds(pl.multiple_of(m * padded, 16), padded)
        for side, rows_ref in ((0, north_rows), (half_slabs, south_rows)):
            for g in range(half_slabs):
                row = held[lax.bitwise_xor(slab, side + g), here, :]
                for f in range(field_here):
                    rows_ref[f * padded : (f + 1) * padded, g * lat_here : (g + 1) * lat_here] = row[
                        :, f * lat_here : (f + 1) * lat_here
                    ]
        north = north_rows[...].astype(jnp.float32)
        south = dot(south_rows[...], mirror_ref[...])
        weight = weight_ref[...]
        wave = (group * slab_count + slab) * wave_here + m
        degree_index = lax.broadcasted_iota(jnp.int32, (1, degree_count), 1)
        returned = []
        for p in range(2):
            both = (north + south) if p == 0 else (north - south)
            paired = (both * weight).astype(jnp.bfloat16)
            spectrum = dot(paired, table_ref[0, p], NT)
            degree = 2 * degree_index + (wave + p) % 2
            ratio = (degree * (degree + 1)).astype(jnp.float32) / float(lat_count * (lat_count - 1))
            damping = 1.0 / (1.0 + rate_ref[...] * (ratio * ratio))
            damping = jnp.where(degree >= wave, damping, 0.0)
            filtered = jnp.concatenate(
                [
                    (spectrum[f * padded : (f + 1) * padded] * damping[f : f + 1]).astype(jnp.bfloat16)
                    for f in range(field_here)
                ],
                axis=0,
            )
            returned.append(dot(filtered, table_ref[0, p]))
        north_rows[...] = (returned[0] + returned[1]).astype(jnp.bfloat16)
        south_rows[...] = dot(
            (returned[0] - returned[1]).astype(jnp.bfloat16), mirror_ref[...]
        ).astype(jnp.bfloat16)
        for side, rows_ref in ((0, north_rows), (half_slabs, south_rows)):
            for g in range(half_slabs):
                at = lax.bitwise_xor(slab, side + g)
                for f in range(field_here):
                    held[at, here, f * lat_here : (f + 1) * lat_here] = rows_ref[
                        f * padded : (f + 1) * padded, g * lat_here : (g + 1) * lat_here
                    ]

        @pl.when(m == wave_here - 1)
        def _():
            for s in range(slab_count):
                out_refs[s][...] = dot(scatter_ref[...], held[s]).astype(jnp.bfloat16)

    def fixed(*dims):
        return pl.BlockSpec(dims, lambda m: (0,) * len(dims), pipeline_mode=pl.Buffered(1))

    rows = survivor_count * row_here
    return pl.pallas_call(
        kernel,
        name="spectral",
        grid=(wave_here,),
        in_specs=[
            pl.BlockSpec(memory_space=pltpu.SMEM),
            fixed(*gather.shape),
            fixed(*scatter.shape),
            fixed(hemisphere, hemisphere),
            fixed(1, hemisphere),
            fixed(field_here, 1),
            pl.BlockSpec((1, 2, degree_count, hemisphere), lambda m: (m, 0, 0, 0)),
        ]
        + [fixed(rows, points)] * slab_count,
        out_specs=[fixed(rows, points)] * slab_count,
        out_shape=[jax.ShapeDtypeStruct((rows, points), jnp.bfloat16)] * slab_count,
        scratch_shapes=[
            pltpu.VMEM((slab_count, wave_here * padded, points), jnp.bfloat16),
            pltpu.VMEM((field_here * padded, hemisphere), jnp.bfloat16),
            pltpu.VMEM((field_here * padded, hemisphere), jnp.bfloat16),
        ],
        compiler_params=params(),
        cost_estimate=cost(
            20 * 10**9, 2 * wave_here * 2 * degree_count * hemisphere + 4 * slab_count * rows * points
        ),
    )(place, gather, scatter, mirror, quad_weight[None, :], rates[:, None], legendre, *sources)


def run(survivor_count, state, survivors, slot_source, legendre, quad_weight, diffusion):
    group_count = lax.axis_size("traj")
    slab_count = lax.axis_size("grid")
    group_index = lax.axis_index("traj")
    slab_index = lax.axis_index("grid")
    member_here, field_count, lat_here, lon_count = state.shape
    wave_count = lon_count // 2
    row_here = 2 * wave_count // (group_count * slab_count)
    field_here = field_count // FIELD_PARTS
    points = field_here * lat_here
    place = jnp.stack([group_index, slab_index]).astype(jnp.int32)

    forward, inverse = trig_tables(lon_count)
    forward = jnp.asarray(forward).reshape(group_count, slab_count * row_here, lon_count)
    inverse = jnp.asarray(inverse).reshape(group_count, slab_count * row_here, lon_count)
    forward = jnp.stack(
        [
            lax.dynamic_index_in_dim(forward, group_index ^ s, 0, keepdims=False)
            for s in range(group_count)
        ]
    )
    state = state.reshape(member_here, FIELD_PARTS, points, lon_count)

    smoothed = None
    for part in range(FIELD_PARTS):
        waves = exchange(analyse(forward, state, part), "traj")
        waves = [w.reshape(member_here, slab_count, row_here, points) for w in waves]
        kept = exchange(keep(place, survivors, waves, survivor_count), "grid")
        kept = [w.reshape(survivor_count * row_here, points) for w in kept]
        rates = diffusion[part * field_here : (part + 1) * field_here]
        back = spectral_filter(
            place, legendre, quad_weight, rates, kept, survivor_count, field_here
        )
        back = exchange([w.reshape(survivor_count, row_here, points) for w in back], "grid")
        slots = exchange(spread(place, slot_source, back, member_here, group_count), "traj")
        slots = [w.reshape(member_here, slab_count * row_here, points) for w in slots]
        smoothed = synthesise(place, inverse, slots, part, FIELD_PARTS, smoothed)
    return smoothed.reshape(member_here, field_count, lat_here, lon_count)


def on_device(state, counts, slot_perm, legendre, quad_weight, diffusion):
    survivors, slot_source = survivor_lists(counts, slot_perm)
    most = counts.shape[0] - MOST_COPIES + 1
    return run(most, state, survivors, slot_source, legendre, quad_weight, diffusion)


def solution(mesh):
    return jax.shard_map(
        on_device,
        mesh=mesh,
        in_specs=(
            P("traj", None, "grid", None),
            P(),
            P(),
            P(("traj", "grid"), None, None, None),
            P(),
            P(),
        ),
        out_specs=P("traj", None, "grid", None),
        check_vma=False,
    )
```

```python
import math

import jax
import jax.numpy as jnp
import numpy as np
from jax import lax
from jax.experimental import pallas as pl
from jax.experimental.pallas import tpu as pltpu
from jax.sharding import PartitionSpec as P

FIELD_PARTS = 3
MOST_COPIES = 4
VMEM_BYTES = 60 * 2**20
NT = (((1,), (1,)), ((), ()))
TN = (((0,), (0,)), ((), ()))


def parent_slots(counts, slot_perm):
    member_count = counts.shape[0]
    position = jnp.arange(member_count, dtype=jnp.int32)
    copy_end = jnp.cumsum(counts)
    copy_parent = jnp.sum((copy_end[None, :] <= position[:, None]).astype(jnp.int32), axis=1)
    landing = (slot_perm[:, None] == position[None, :]).astype(jnp.int32)
    return jnp.sum(landing * copy_parent[:, None], axis=0)


def survivor_lists(counts, slot_perm):
    member_count = counts.shape[0]
    position = jnp.arange(member_count, dtype=jnp.int32)
    alive = counts > 0
    rank = jnp.sum((position[None, :] < position[:, None]) & alive[None, :], axis=1).astype(jnp.int32)
    hit = alive[None, :] & (rank[None, :] == position[:, None])
    survivors = jnp.sum(hit * position[None, :], axis=1).astype(jnp.int32)
    parents = parent_slots(counts, slot_perm)
    slot_source = jnp.sum((parents[:, None] == position[None, :]) * rank[None, :], axis=1)
    return survivors, slot_source.astype(jnp.int32)


def trig_tables(lon_count):
    wave_count = lon_count // 2
    turn = np.arange(wave_count)[:, None] * np.arange(lon_count)[None, :] % lon_count
    phase = (turn.astype(np.float32) * np.float32(2.0 * math.pi / lon_count)).astype(np.float64)
    pair = np.stack([np.cos(phase), -np.sin(phase)], axis=1).astype(np.float32)
    doubled = np.where(np.arange(wave_count) == 0, 1.0, 2.0).astype(np.float32)
    forward = (pair / np.float32(lon_count)).astype(jnp.bfloat16)
    inverse = (pair * doubled[:, None, None]).astype(jnp.bfloat16)
    return forward.reshape(2 * wave_count, lon_count), inverse.reshape(2 * wave_count, lon_count)


def exchange(pieces, axis):
    size = lax.axis_size(axis)
    out = [pieces[0]]
    for s in range(1, size):
        out.append(lax.ppermute(pieces[s], axis, [(i, i ^ s) for i in range(size)]))
    return out


def params():
    return pltpu.CompilerParams(vmem_limit_bytes=VMEM_BYTES)


def cost(flops, bytes_accessed):
    return pl.CostEstimate(flops=flops, bytes_accessed=bytes_accessed, transcendentals=0)


def dot(a, b, dims=(((1,), (0,)), ((), ()))):
    return lax.dot_general(a, b, dims, preferred_element_type=jnp.float32)


def analyse(table, state, part):
    group_count, rows, lon_count = table.shape
    member_here, _, points, _ = state.shape

    def kernel(table_ref, state_ref, *out_refs):
        block = state_ref[0, 0]
        for s in range(group_count):
            out_refs[s][0] = dot(table_ref[s], block, NT).astype(jnp.bfloat16)

    return pl.pallas_call(
        kernel,
        name="analyse",
        grid=(member_here,),
        in_specs=[
            pl.BlockSpec((group_count, rows, lon_count), lambda t: (0, 0, 0)),
            pl.BlockSpec((1, 1, points, lon_count), lambda t: (t, part, 0, 0)),
        ],
        out_specs=[pl.BlockSpec((1, rows, points), lambda t: (t, 0, 0))] * group_count,
        out_shape=[jax.ShapeDtypeStruct((member_here, rows, points), jnp.bfloat16)] * group_count,
        compiler_params=params(),
        cost_estimate=cost(
            2 * member_here * group_count * rows * lon_count * points,
            2 * member_here * points * (lon_count + group_count * rows),
        ),
    )(table, state)


def keep(place, survivors, sources, survivor_count):
    group_count = len(sources)
    member_here, slab_count, rows, points = sources[0].shape
    survivors = survivors[:survivor_count]
    offset = survivors // member_here ^ place[0]
    step = jnp.arange(survivor_count, dtype=jnp.int32)
    seen = (offset[None, None, :] == jnp.arange(group_count, dtype=jnp.int32)[:, None, None]) & (
        step[None, None, :] <= step[None, :, None]
    )
    shown = jnp.max(jnp.where(seen, survivors % member_here, 0), axis=2).reshape(-1)

    def kernel(place_ref, offset_ref, shown_ref, *refs):
        source_refs = refs[:group_count]
        out_refs = refs[group_count:]
        slab = place_ref[1]
        chosen = offset_ref[pl.program_id(0)]
        for k in range(group_count):

            @pl.when(chosen == k)
            def _(k=k):
                for s in range(slab_count):
                    out_refs[s][0] = source_refs[k][0, lax.bitwise_xor(slab, s)]

    return pl.pallas_call(
        kernel,
        name="keep",
        grid_spec=pltpu.PrefetchScalarGridSpec(
            num_scalar_prefetch=3,
            grid=(survivor_count,),
            in_specs=[
                pl.BlockSpec(
                    (1, slab_count, rows, points),
                    lambda d, place_ref, offset_ref, shown_ref, k=k: (
                        shown_ref[k * survivor_count + d],
                        0,
                        0,
                        0,
                    ),
                )
                for k in range(group_count)
            ],
            out_specs=[pl.BlockSpec((1, rows, points), lambda d, *_: (d, 0, 0))] * slab_count,
        ),
        out_shape=[jax.ShapeDtypeStruct((survivor_count, rows, points), jnp.bfloat16)] * slab_count,
        compiler_params=params(),
        cost_estimate=cost(0, 4 * survivor_count * slab_count * rows * points),
    )(place, offset, shown, *sources)


def spread(place, slot_source, sources, member_here, group_count):
    slab_count = len(sources)
    _, rows, points = sources[0].shape

    def source_at(k, t, place_ref, slot_ref):
        return slot_ref[lax.bitwise_xor(place_ref[0], k) * member_here + t], 0, 0

    def kernel(place_ref, slot_ref, *refs):
        source_refs = refs[:slab_count]
        out_refs = refs[slab_count:]
        slab = place_ref[1]
        for k in range(group_count):

            @pl.when(pl.program_id(0) == k)
            def _(k=k):
                for s in range(slab_count):
                    out_refs[k][0, lax.bitwise_xor(slab, s)] = source_refs[s][0]

    return pl.pallas_call(
        kernel,
        name="spread",
        grid_spec=pltpu.PrefetchScalarGridSpec(
            num_scalar_prefetch=2,
            grid=(group_count, member_here),
            in_specs=[pl.BlockSpec((1, rows, points), source_at)] * slab_count,
            out_specs=[
                pl.BlockSpec(
                    (1, slab_count, rows, points),
                    lambda k, t, *_, own=own: (
                        jnp.where(k == own, t, jnp.where(k < own, 0, member_here - 1)),
                        0,
                        0,
                        0,
                    ),
                )
                for own in range(group_count)
            ],
        ),
        out_shape=[
            jax.ShapeDtypeStruct((member_here, slab_count, rows, points), jnp.bfloat16)
        ]
        * group_count,
        compiler_params=params(),
        cost_estimate=cost(0, 4 * group_count * member_here * slab_count * rows * points),
    )(place, slot_source, *sources)


def synthesise(place, table, sources, part, part_count, earlier):
    group_count, rows, lon_count = table.shape
    member_here, _, points = sources[0].shape

    def kernel(place_ref, table_ref, *refs):
        group = place_ref[0]
        total = dot(refs[0][0], table_ref[group], TN)
        for s in range(1, group_count):
            total += dot(refs[s][0], table_ref[lax.bitwise_xor(group, s)], TN)
        refs[-1][0, 0] = total.astype(jnp.bfloat16)

    given = [place, table, *sources]
    specs = [
        pl.BlockSpec(memory_space=pltpu.SMEM),
        pl.BlockSpec((group_count, rows, lon_count), lambda t: (0, 0, 0)),
    ] + [pl.BlockSpec((1, rows, points), lambda t: (t, 0, 0))] * group_count
    aliases = {}
    if earlier is not None:
        aliases = {len(given): 0}
        given.append(earlier)
        specs.append(pl.BlockSpec(memory_space=pl.ANY))
    return pl.pallas_call(
        kernel,
        name="synthesise",
        grid=(member_here,),
        in_specs=specs,
        out_specs=pl.BlockSpec((1, 1, points, lon_count), lambda t: (t, part, 0, 0)),
        out_shape=jax.ShapeDtypeStruct((member_here, part_count, points, lon_count), jnp.bfloat16),
        input_output_aliases=aliases,
        compiler_params=params(),
        cost_estimate=cost(
            2 * member_here * group_count * rows * lon_count * points,
            2 * member_here * points * (lon_count + group_count * rows),
        ),
    )(*given)


def spectral_filter(place, legendre, quad_weight, rates, sources, survivor_count, field_here):
    slab_count = len(sources)
    points = sources[0].shape[1]
    lat_here = points // field_here
    wave_here, _, degree_count, hemisphere = legendre.shape
    lat_count = 2 * hemisphere
    half_slabs = slab_count // 2
    row_here = 2 * wave_here
    used = 2 * survivor_count
    padded = -(-used // 16) * 16

    shuffle = np.zeros((wave_here, padded, survivor_count, wave_here, 2), np.float32)
    for m in range(wave_here):
        for d in range(survivor_count):
            for r in range(2):
                shuffle[m, 2 * d + r, d, m, r] = 1.0
    shuffle = shuffle.reshape(wave_here * padded, survivor_count * row_here)
    gather = jnp.asarray(shuffle.astype(jnp.bfloat16))
    scatter = jnp.asarray(shuffle.T.astype(jnp.bfloat16))
    mirror = jnp.asarray(np.eye(hemisphere, dtype=np.float32)[::-1].astype(jnp.bfloat16))

    def kernel(place_ref, gather_ref, scatter_ref, mirror_ref, weight_ref, rate_ref, table_ref, *refs):
        source_refs = refs[:slab_count]
        out_refs = refs[slab_count : 2 * slab_count]
        held, north_rows, south_rows = refs[2 * slab_count :]
        m = pl.program_id(0)
        group, slab = place_ref[0], place_ref[1]

        @pl.when(m == 0)
        def _():
            for s in range(slab_count):
                held[s] = dot(gather_ref[...], source_refs[s][...]).astype(jnp.bfloat16)

        here = pl.ds(pl.multiple_of(m * padded, 16), padded)
        for side, rows_ref in ((0, north_rows), (half_slabs, south_rows)):
            for g in range(half_slabs):
                row = held[lax.bitwise_xor(slab, side + g), here, :]
                for f in range(field_here):
                    rows_ref[f * padded : (f + 1) * padded, g * lat_here : (g + 1) * lat_here] = row[
                        :, f * lat_here : (f + 1) * lat_here
                    ]
        north = north_rows[...].astype(jnp.float32)
        south = dot(south_rows[...], mirror_ref[...])
        weight = weight_ref[...]
        wave = (group * slab_count + slab) * wave_here + m
        degree_index = lax.broadcasted_iota(jnp.int32, (1, degree_count), 1)
        returned = []
        for p in range(2):
            both = (north + south) if p == 0 else (north - south)
            paired = (both * weight).astype(jnp.bfloat16)
            spectrum = dot(paired, table_ref[0, p], NT)
            degree = 2 * degree_index + (wave + p) % 2
            ratio = (degree * (degree + 1)).astype(jnp.float32) / float(lat_count * (lat_count - 1))
            damping = 1.0 / (1.0 + rate_ref[...] * (ratio * ratio))
            damping = jnp.where(degree >= wave, damping, 0.0)
            filtered = jnp.concatenate(
                [
                    (spectrum[f * padded : (f + 1) * padded] * damping[f : f + 1]).astype(jnp.bfloat16)
                    for f in range(field_here)
                ],
                axis=0,
            )
            returned.append(dot(filtered, table_ref[0, p]))
        north_rows[...] = (returned[0] + returned[1]).astype(jnp.bfloat16)
        south_rows[...] = dot(
            (returned[0] - returned[1]).astype(jnp.bfloat16), mirror_ref[...]
        ).astype(jnp.bfloat16)
        for side, rows_ref in ((0, north_rows), (half_slabs, south_rows)):
            for g in range(half_slabs):
                at = lax.bitwise_xor(slab, side + g)
                for f in range(field_here):
                    held[at, here, f * lat_here : (f + 1) * lat_here] = rows_ref[
                        f * padded : (f + 1) * padded, g * lat_here : (g + 1) * lat_here
                    ]

        @pl.when(m == wave_here - 1)
        def _():
            for s in range(slab_count):
                out_refs[s][...] = dot(scatter_ref[...], held[s]).astype(jnp.bfloat16)

    def fixed(*dims):
        return pl.BlockSpec(dims, lambda m: (0,) * len(dims), pipeline_mode=pl.Buffered(1))

    rows = survivor_count * row_here
    return pl.pallas_call(
        kernel,
        name="spectral",
        grid=(wave_here,),
        in_specs=[
            pl.BlockSpec(memory_space=pltpu.SMEM),
            fixed(*gather.shape),
            fixed(*scatter.shape),
            fixed(hemisphere, hemisphere),
            fixed(1, hemisphere),
            fixed(field_here, 1),
            pl.BlockSpec((1, 2, degree_count, hemisphere), lambda m: (m, 0, 0, 0)),
        ]
        + [fixed(rows, points)] * slab_count,
        out_specs=[fixed(rows, points)] * slab_count,
        out_shape=[jax.ShapeDtypeStruct((rows, points), jnp.bfloat16)] * slab_count,
        scratch_shapes=[
            pltpu.VMEM((slab_count, wave_here * padded, points), jnp.bfloat16),
            pltpu.VMEM((field_here * padded, hemisphere), jnp.bfloat16),
            pltpu.VMEM((field_here * padded, hemisphere), jnp.bfloat16),
        ],
        compiler_params=params(),
        cost_estimate=cost(
            20 * 10**9, 2 * wave_here * 2 * degree_count * hemisphere + 4 * slab_count * rows * points
        ),
    )(place, gather, scatter, mirror, quad_weight[None, :], rates[:, None], legendre, *sources)


def run(survivor_count, state, survivors, slot_source, legendre, quad_weight, diffusion):
    group_count = lax.axis_size("traj")
    slab_count = lax.axis_size("grid")
    group_index = lax.axis_index("traj")
    slab_index = lax.axis_index("grid")
    member_here, field_count, lat_here, lon_count = state.shape
    wave_count = lon_count // 2
    row_here = 2 * wave_count // (group_count * slab_count)
    field_here = field_count // FIELD_PARTS
    points = field_here * lat_here
    place = jnp.stack([group_index, slab_index]).astype(jnp.int32)

    forward, inverse = trig_tables(lon_count)
    forward = jnp.asarray(forward).reshape(group_count, slab_count * row_here, lon_count)
    inverse = jnp.asarray(inverse).reshape(group_count, slab_count * row_here, lon_count)
    forward = jnp.stack(
        [
            lax.dynamic_index_in_dim(forward, group_index ^ s, 0, keepdims=False)
            for s in range(group_count)
        ]
    )
    state = state.reshape(member_here, FIELD_PARTS, points, lon_count)

    smoothed = None
    for part in range(FIELD_PARTS):
        waves = exchange(analyse(forward, state, part), "traj")
        waves = [w.reshape(member_here, slab_count, row_here, points) for w in waves]
        kept = exchange(keep(place, survivors, waves, survivor_count), "grid")
        kept = [w.reshape(survivor_count * row_here, points) for w in kept]
        rates = diffusion[part * field_here : (part + 1) * field_here]
        back = spectral_filter(
            place, legendre, quad_weight, rates, kept, survivor_count, field_here
        )
        back = exchange([w.reshape(survivor_count, row_here, points) for w in back], "grid")
        slots = exchange(spread(place, slot_source, back, member_here, group_count), "traj")
        slots = [w.reshape(member_here, slab_count * row_here, points) for w in slots]
        smoothed = synthesise(place, inverse, slots, part, FIELD_PARTS, smoothed)
    return smoothed.reshape(member_here, field_count, lat_here, lon_count)


def on_device(state, counts, slot_perm, legendre, quad_weight, diffusion):
    survivors, slot_source = survivor_lists(counts, slot_perm)
    most = counts.shape[0] - MOST_COPIES + 1
    return run(most, state, survivors, slot_source, legendre, quad_weight, diffusion)


def solution(mesh):
    return jax.shard_map(
        on_device,
        mesh=mesh,
        in_specs=(
            P("traj", None, "grid", None),
            P(),
            P(),
            P(("traj", "grid"), None, None, None),
            P(),
            P(),
        ),
        out_specs=P("traj", None, "grid", None),
        check_vma=False,
    )
```

```python
import functools
import math

import jax
import jax.numpy as jnp
import numpy as np
from jax import lax
from jax.experimental import pallas as pl
from jax.experimental.pallas import tpu as pltpu
from jax.sharding import PartitionSpec as P

FIELD_PARTS = 3
MOST_COPIES = 4
LEAST_ROWS = 8
VMEM_BYTES = 60 * 2**20
NT = (((1,), (1,)), ((), ()))
TN = (((0,), (0,)), ((), ()))


def parent_slots(counts, slot_perm):
    member_count = counts.shape[0]
    position = jnp.arange(member_count, dtype=jnp.int32)
    copy_end = jnp.cumsum(counts)
    copy_parent = jnp.sum((copy_end[None, :] <= position[:, None]).astype(jnp.int32), axis=1)
    landing = (slot_perm[:, None] == position[None, :]).astype(jnp.int32)
    return jnp.sum(landing * copy_parent[:, None], axis=0)


def survivor_lists(counts, slot_perm):
    member_count = counts.shape[0]
    position = jnp.arange(member_count, dtype=jnp.int32)
    alive = counts > 0
    rank = jnp.sum((position[None, :] < position[:, None]) & alive[None, :], axis=1).astype(jnp.int32)
    hit = alive[None, :] & (rank[None, :] == position[:, None])
    survivors = jnp.sum(hit * position[None, :], axis=1).astype(jnp.int32)
    parents = parent_slots(counts, slot_perm)
    slot_source = jnp.sum((parents[:, None] == position[None, :]) * rank[None, :], axis=1)
    return survivors, slot_source.astype(jnp.int32)


def trig_tables(lon_count):
    wave_count = lon_count // 2
    turn = np.arange(wave_count)[:, None] * np.arange(lon_count)[None, :] % lon_count
    phase = (turn.astype(np.float32) * np.float32(2.0 * math.pi / lon_count)).astype(np.float64)
    pair = np.stack([np.cos(phase), -np.sin(phase)], axis=1).astype(np.float32)
    doubled = np.where(np.arange(wave_count) == 0, 1.0, 2.0).astype(np.float32)
    forward = (pair / np.float32(lon_count)).astype(jnp.bfloat16)
    inverse = (pair * doubled[:, None, None]).astype(jnp.bfloat16)
    return forward.reshape(2 * wave_count, lon_count), inverse.reshape(2 * wave_count, lon_count)


def exchange(pieces, axis):
    size = lax.axis_size(axis)
    out = [pieces[0]]
    for s in range(1, size):
        out.append(lax.ppermute(pieces[s], axis, [(i, i ^ s) for i in range(size)]))
    return out


def transpose(blocks):
    return lax.all_to_all(blocks, "grid", split_axis=0, concat_axis=0, tiled=True)


def params():
    return pltpu.CompilerParams(vmem_limit_bytes=VMEM_BYTES)


def cost(flops, bytes_accessed):
    return pl.CostEstimate(flops=flops, bytes_accessed=bytes_accessed, transcendentals=0)


def dot(a, b, dims=(((1,), (0,)), ((), ()))):
    return lax.dot_general(a, b, dims, preferred_element_type=jnp.float32)


def analyse(table, state, part):
    group_count, rows, lon_count = table.shape
    member_here, _, points, _ = state.shape

    def kernel(table_ref, state_ref, *out_refs):
        block = state_ref[0, 0]
        for s in range(group_count):
            out_refs[s][0] = dot(table_ref[s], block, NT).astype(jnp.bfloat16)

    return pl.pallas_call(
        kernel,
        name="analyse",
        grid=(member_here,),
        in_specs=[
            pl.BlockSpec((group_count, rows, lon_count), lambda t: (0, 0, 0)),
            pl.BlockSpec((1, 1, points, lon_count), lambda t: (t, part, 0, 0)),
        ],
        out_specs=[pl.BlockSpec((1, rows, points), lambda t: (t, 0, 0))] * group_count,
        out_shape=[jax.ShapeDtypeStruct((member_here, rows, points), jnp.bfloat16)] * group_count,
        compiler_params=params(),
        cost_estimate=cost(
            2 * member_here * group_count * rows * lon_count * points,
            2 * member_here * points * (lon_count + group_count * rows),
        ),
    )(table, state)


def keep(place, survivors, sources, survivor_count):
    group_count = len(sources)
    member_here, slab_count, rows, points = sources[0].shape
    survivors = survivors[:survivor_count]
    offset = survivors // member_here ^ place[0]
    step = jnp.arange(survivor_count, dtype=jnp.int32)
    seen = (offset[None, None, :] == jnp.arange(group_count, dtype=jnp.int32)[:, None, None]) & (
        step[None, None, :] <= step[None, :, None]
    )
    shown = jnp.max(jnp.where(seen, survivors % member_here, 0), axis=2).reshape(-1)

    def kernel(offset_ref, shown_ref, *refs):
        out_ref = refs[-1]
        chosen = offset_ref[pl.program_id(0)]
        for k in range(group_count):

            @pl.when(chosen == k)
            def _(k=k):
                out_ref[:, 0] = refs[k][0]

    return pl.pallas_call(
        kernel,
        name="keep",
        grid_spec=pltpu.PrefetchScalarGridSpec(
            num_scalar_prefetch=2,
            grid=(survivor_count,),
            in_specs=[
                pl.BlockSpec(
                    (1, slab_count, rows, points),
                    lambda d, offset_ref, shown_ref, k=k: (
                        shown_ref[k * survivor_count + d],
                        0,
                        0,
                        0,
                    ),
                )
                for k in range(group_count)
            ],
            out_specs=pl.BlockSpec((slab_count, 1, rows, points), lambda d, *_: (0, d, 0, 0)),
        ),
        out_shape=jax.ShapeDtypeStruct((slab_count, survivor_count, rows, points), jnp.bfloat16),
        compiler_params=params(),
        cost_estimate=cost(0, 4 * survivor_count * slab_count * rows * points),
    )(offset, shown, *sources)


def spread(place, slot_source, source, member_here, group_count):
    slab_count, _, rows, points = source.shape

    def source_at(k, t, place_ref, slot_ref):
        return 0, slot_ref[lax.bitwise_xor(place_ref[0], k) * member_here + t], 0, 0

    def kernel(place_ref, slot_ref, source_ref, *out_refs):
        for k in range(group_count):

            @pl.when(pl.program_id(0) == k)
            def _(k=k):
                out_refs[k][0] = source_ref[:, 0]

    return pl.pallas_call(
        kernel,
        name="spread",
        grid_spec=pltpu.PrefetchScalarGridSpec(
            num_scalar_prefetch=2,
            grid=(group_count, member_here),
            in_specs=[pl.BlockSpec((slab_count, 1, rows, points), source_at)],
            out_specs=[
                pl.BlockSpec(
                    (1, slab_count, rows, points),
                    lambda k, t, *_, own=own: (
                        jnp.where(k == own, t, jnp.where(k < own, 0, member_here - 1)),
                        0,
                        0,
                        0,
                    ),
                )
                for own in range(group_count)
            ],
        ),
        out_shape=[
            jax.ShapeDtypeStruct((member_here, slab_count, rows, points), jnp.bfloat16)
        ]
        * group_count,
        compiler_params=params(),
        cost_estimate=cost(0, 4 * group_count * member_here * slab_count * rows * points),
    )(place, slot_source, source)


def synthesise(place, table, sources, part, part_count, earlier):
    group_count, rows, lon_count = table.shape
    member_here, _, points = sources[0].shape

    def kernel(place_ref, table_ref, *refs):
        group = place_ref[0]
        total = dot(refs[0][0], table_ref[group], TN)
        for s in range(1, group_count):
            total += dot(refs[s][0], table_ref[lax.bitwise_xor(group, s)], TN)
        refs[-1][0, 0] = total.astype(jnp.bfloat16)

    given = [place, table, *sources]
    specs = [
        pl.BlockSpec(memory_space=pltpu.SMEM),
        pl.BlockSpec((group_count, rows, lon_count), lambda t: (0, 0, 0)),
    ] + [pl.BlockSpec((1, rows, points), lambda t: (t, 0, 0))] * group_count
    aliases = {}
    if earlier is not None:
        aliases = {len(given): 0}
        given.append(earlier)
        specs.append(pl.BlockSpec(memory_space=pl.ANY))
    return pl.pallas_call(
        kernel,
        name="synthesise",
        grid=(member_here,),
        in_specs=specs,
        out_specs=pl.BlockSpec((1, 1, points, lon_count), lambda t: (t, part, 0, 0)),
        out_shape=jax.ShapeDtypeStruct((member_here, part_count, points, lon_count), jnp.bfloat16),
        input_output_aliases=aliases,
        compiler_params=params(),
        cost_estimate=cost(
            2 * member_here * group_count * rows * lon_count * points,
            2 * member_here * points * (lon_count + group_count * rows),
        ),
    )(*given)


def spectral_filter(place, legendre, quad_weight, rates, source, survivor_count, field_here):
    slab_count, rows, points = source.shape
    lat_here = points // field_here
    wave_here, _, degree_count, hemisphere = legendre.shape
    lat_count = 2 * hemisphere
    half_slabs = slab_count // 2
    row_here = 2 * wave_here
    used = 2 * survivor_count
    padded = -(-used // 16) * 16

    shuffle = np.zeros((wave_here, padded, survivor_count, wave_here, 2), np.float32)
    for m in range(wave_here):
        for d in range(survivor_count):
            for r in range(2):
                shuffle[m, 2 * d + r, d, m, r] = 1.0
    shuffle = shuffle.reshape(wave_here * padded, survivor_count * row_here)
    gather = jnp.asarray(shuffle.astype(jnp.bfloat16))
    scatter = jnp.asarray(shuffle.T.astype(jnp.bfloat16))
    mirror = jnp.asarray(np.eye(hemisphere, dtype=np.float32)[::-1].astype(jnp.bfloat16))

    def kernel(
        place_ref,
        gather_ref,
        scatter_ref,
        mirror_ref,
        weight_ref,
        rate_ref,
        table_ref,
        source_ref,
        out_ref,
        held,
        north_rows,
        south_rows,
    ):
        m = pl.program_id(0)
        group, slab = place_ref[0], place_ref[1]

        @pl.when(m == 0)
        def _():
            for s in range(slab_count):
                held[s] = dot(gather_ref[...], source_ref[s]).astype(jnp.bfloat16)

        here = pl.ds(pl.multiple_of(m * padded, 16), padded)
        for side, rows_ref in ((0, north_rows), (half_slabs, south_rows)):
            for g in range(half_slabs):
                row = held[side + g, here, :]
                for f in range(field_here):
                    rows_ref[f * padded : (f + 1) * padded, g * lat_here : (g + 1) * lat_here] = row[
                        :, f * lat_here : (f + 1) * lat_here
                    ]
        north = north_rows[...].astype(jnp.float32)
        south = dot(south_rows[...], mirror_ref[...])
        weight = weight_ref[...]
        wave = (group * slab_count + slab) * wave_here + m
        degree_index = lax.broadcasted_iota(jnp.int32, (1, degree_count), 1)
        returned = []
        for p in range(2):
            both = (north + south) if p == 0 else (north - south)
            paired = (both * weight).astype(jnp.bfloat16)
            spectrum = dot(paired, table_ref[0, p], NT)
            degree = 2 * degree_index + (wave + p) % 2
            ratio = (degree * (degree + 1)).astype(jnp.float32) / float(lat_count * (lat_count - 1))
            damping = 1.0 / (1.0 + rate_ref[...] * (ratio * ratio))
            damping = jnp.where(degree >= wave, damping, 0.0)
            filtered = jnp.concatenate(
                [
                    (spectrum[f * padded : (f + 1) * padded] * damping[f : f + 1]).astype(jnp.bfloat16)
                    for f in range(field_here)
                ],
                axis=0,
            )
            returned.append(dot(filtered, table_ref[0, p]))
        north_rows[...] = (returned[0] + returned[1]).astype(jnp.bfloat16)
        south_rows[...] = dot(
            (returned[0] - returned[1]).astype(jnp.bfloat16), mirror_ref[...]
        ).astype(jnp.bfloat16)
        for side, rows_ref in ((0, north_rows), (half_slabs, south_rows)):
            for g in range(half_slabs):
                for f in range(field_here):
                    held[side + g, here, f * lat_here : (f + 1) * lat_here] = rows_ref[
                        f * padded : (f + 1) * padded, g * lat_here : (g + 1) * lat_here
                    ]

        @pl.when(m == wave_here - 1)
        def _():
            for s in range(slab_count):
                out_ref[s] = dot(scatter_ref[...], held[s]).astype(jnp.bfloat16)

    def fixed(*dims):
        return pl.BlockSpec(dims, lambda m: (0,) * len(dims), pipeline_mode=pl.Buffered(1))

    return pl.pallas_call(
        kernel,
        name="spectral",
        grid=(wave_here,),
        in_specs=[
            pl.BlockSpec(memory_space=pltpu.SMEM),
            fixed(*gather.shape),
            fixed(*scatter.shape),
            fixed(hemisphere, hemisphere),
            fixed(1, hemisphere),
            fixed(field_here, 1),
            pl.BlockSpec((1, 2, degree_count, hemisphere), lambda m: (m, 0, 0, 0)),
        ]
        + [fixed(slab_count, rows, points)],
        out_specs=fixed(slab_count, rows, points),
        out_shape=jax.ShapeDtypeStruct((slab_count, rows, points), jnp.bfloat16),
        scratch_shapes=[
            pltpu.VMEM((slab_count, wave_here * padded, points), jnp.bfloat16),
            pltpu.VMEM((field_here * padded, hemisphere), jnp.bfloat16),
            pltpu.VMEM((field_here * padded, hemisphere), jnp.bfloat16),
        ],
        compiler_params=params(),
        cost_estimate=cost(
            20 * 10**9, 2 * wave_here * 2 * degree_count * hemisphere + 4 * slab_count * rows * points
        ),
    )(place, gather, scatter, mirror, quad_weight[None, :], rates[:, None], legendre, source)


def run(
    survivor_count, state, forward, inverse, survivors, slot_source, legendre, quad_weight, diffusion
):
    group_count = lax.axis_size("traj")
    slab_count = lax.axis_size("grid")
    place = jnp.stack([lax.axis_index("traj"), lax.axis_index("grid")]).astype(jnp.int32)
    member_here, _, points, lon_count = state.shape
    row_here = lon_count // (group_count * slab_count)
    field_here = diffusion.shape[0] // FIELD_PARTS

    smoothed = None
    for part in range(FIELD_PARTS):
        waves = exchange(analyse(forward, state, part), "traj")
        waves = [w.reshape(member_here, slab_count, row_here, points) for w in waves]
        kept = transpose(keep(place, survivors, waves, survivor_count))
        kept = kept.reshape(slab_count, survivor_count * row_here, points)
        rates = diffusion[part * field_here : (part + 1) * field_here]
        back = spectral_filter(
            place, legendre, quad_weight, rates, kept, survivor_count, field_here
        )
        back = transpose(back.reshape(slab_count, survivor_count, row_here, points))
        slots = exchange(spread(place, slot_source, back, member_here, group_count), "traj")
        slots = [w.reshape(member_here, slab_count * row_here, points) for w in slots]
        smoothed = synthesise(place, inverse, slots, part, FIELD_PARTS, smoothed)
    return smoothed


def on_device(state, counts, slot_perm, legendre, quad_weight, diffusion):
    survivors, slot_source = survivor_lists(counts, slot_perm)
    group_count = lax.axis_size("traj")
    group_index = lax.axis_index("traj")
    member_here, field_count, lat_here, lon_count = state.shape
    forward, inverse = trig_tables(lon_count)
    forward = jnp.asarray(forward).reshape(group_count, -1, lon_count)
    inverse = jnp.asarray(inverse).reshape(group_count, -1, lon_count)
    forward = jnp.stack(
        [
            lax.dynamic_index_in_dim(forward, group_index ^ s, 0, keepdims=False)
            for s in range(group_count)
        ]
    )
    parts = state.reshape(member_here, FIELD_PARTS, -1, lon_count)
    most = counts.shape[0] - MOST_COPIES + 1
    sizes = range(min(LEAST_ROWS, most), most + 1)
    branch = jnp.clip(jnp.sum(counts > 0).astype(jnp.int32) - sizes[0], 0, len(sizes) - 1)
    smoothed = lax.switch(
        branch,
        [functools.partial(run, size) for size in sizes],
        parts,
        forward,
        inverse,
        survivors,
        slot_source,
        legendre,
        quad_weight,
        diffusion,
    )
    return smoothed.reshape(member_here, field_count, lat_here, lon_count)


def solution(mesh):
    return jax.shard_map(
        on_device,
        mesh=mesh,
        in_specs=(
            P("traj", None, "grid", None),
            P(),
            P(),
            P(("traj", "grid"), None, None, None),
            P(),
            P(),
        ),
        out_specs=P("traj", None, "grid", None),
        check_vma=False,
    )
```

```python
import functools
import math

import jax
import jax.numpy as jnp
import numpy as np
from jax import lax
from jax.experimental import pallas as pl
from jax.experimental.pallas import tpu as pltpu
from jax.sharding import PartitionSpec as P

FIELD_PARTS = 3
MOST_COPIES = 4
LEAST_ROWS = 8
VMEM_BYTES = 60 * 2**20
NT = (((1,), (1,)), ((), ()))
TN = (((0,), (0,)), ((), ()))


def parent_slots(counts, slot_perm):
    member_count = counts.shape[0]
    position = jnp.arange(member_count, dtype=jnp.int32)
    copy_end = jnp.cumsum(counts)
    copy_parent = jnp.sum((copy_end[None, :] <= position[:, None]).astype(jnp.int32), axis=1)
    landing = (slot_perm[:, None] == position[None, :]).astype(jnp.int32)
    return jnp.sum(landing * copy_parent[:, None], axis=0)


def survivor_lists(counts, slot_perm):
    member_count = counts.shape[0]
    position = jnp.arange(member_count, dtype=jnp.int32)
    alive = counts > 0
    rank = jnp.sum((position[None, :] < position[:, None]) & alive[None, :], axis=1).astype(jnp.int32)
    hit = alive[None, :] & (rank[None, :] == position[:, None])
    survivors = jnp.sum(hit * position[None, :], axis=1).astype(jnp.int32)
    parents = parent_slots(counts, slot_perm)
    slot_source = jnp.sum((parents[:, None] == position[None, :]) * rank[None, :], axis=1)
    return survivors, slot_source.astype(jnp.int32)


def trig_tables(lon_count):
    wave_count = lon_count // 2
    turn = np.arange(wave_count)[:, None] * np.arange(lon_count)[None, :] % lon_count
    phase = (turn.astype(np.float32) * np.float32(2.0 * math.pi / lon_count)).astype(np.float64)
    pair = np.stack([np.cos(phase), -np.sin(phase)], axis=1).astype(np.float32)
    doubled = np.where(np.arange(wave_count) == 0, 1.0, 2.0).astype(np.float32)
    forward = (pair / np.float32(lon_count)).astype(jnp.bfloat16)
    inverse = (pair * doubled[:, None, None]).astype(jnp.bfloat16)
    return forward.reshape(2 * wave_count, lon_count), inverse.reshape(2 * wave_count, lon_count)


def exchange(pieces, axis):
    size = lax.axis_size(axis)
    out = [pieces[0]]
    for s in range(1, size):
        out.append(lax.ppermute(pieces[s], axis, [(i, i ^ s) for i in range(size)]))
    return out


def transpose(blocks):
    return lax.all_to_all(blocks, "grid", split_axis=0, concat_axis=0, tiled=True)


def params():
    return pltpu.CompilerParams(vmem_limit_bytes=VMEM_BYTES)


def cost(flops, bytes_accessed):
    return pl.CostEstimate(flops=flops, bytes_accessed=bytes_accessed, transcendentals=0)


def dot(a, b, dims=(((1,), (0,)), ((), ()))):
    return lax.dot_general(a, b, dims, preferred_element_type=jnp.float32)


def analyse(place, table, state, part, cut):
    group_count, rows, lon_count = table.shape
    member_here, _, fields, lats, _ = state.shape
    points = fields * (cut[1] - cut[0])

    def kernel(place_ref, table_ref, state_ref, *out_refs):
        group = place_ref[0]
        block = state_ref[0, 0, :, cut[0] : cut[1], :].reshape(points, lon_count)
        for s in range(group_count):
            out_refs[s][0] = dot(table_ref[lax.bitwise_xor(group, s)], block, NT).astype(jnp.bfloat16)

    return pl.pallas_call(
        kernel,
        name="analyse",
        grid=(member_here,),
        in_specs=[
            pl.BlockSpec(memory_space=pltpu.SMEM),
            pl.BlockSpec((group_count, rows, lon_count), lambda t: (0, 0, 0)),
            pl.BlockSpec((1, 1, fields, lats, lon_count), lambda t: (t, part, 0, 0, 0)),
        ],
        out_specs=[pl.BlockSpec((1, rows, points), lambda t: (t, 0, 0))] * group_count,
        out_shape=[jax.ShapeDtypeStruct((member_here, rows, points), jnp.bfloat16)] * group_count,
        compiler_params=params(),
        cost_estimate=cost(
            2 * member_here * group_count * rows * lon_count * points,
            2 * member_here * points * (lon_count + group_count * rows),
        ),
    )(place, table, state)


def keep(place, survivors, sources, survivor_count, later, before):
    group_count = len(sources)
    member_here, slab_count, rows, points = sources[0].shape
    survivors = survivors[:survivor_count]
    offset = survivors // member_here ^ place[0]
    step = jnp.arange(survivor_count, dtype=jnp.int32)
    seen = (offset[None, None, :] == jnp.arange(group_count, dtype=jnp.int32)[:, None, None]) & (
        step[None, None, :] <= step[None, :, None]
    )
    shown = jnp.max(jnp.where(seen, survivors % member_here, 0), axis=2).reshape(-1)

    def kernel(offset_ref, shown_ref, *refs):
        out_ref = refs[group_count + len(later) + len(before)]
        chosen = offset_ref[pl.program_id(0)]
        for k in range(group_count):

            @pl.when(chosen == k)
            def _(k=k):
                out_ref[:, 0] = refs[k][0]

    return pl.pallas_call(
        kernel,
        name="keep",
        grid_spec=pltpu.PrefetchScalarGridSpec(
            num_scalar_prefetch=2,
            grid=(survivor_count,),
            in_specs=[
                pl.BlockSpec(
                    (1, slab_count, rows, points),
                    lambda d, offset_ref, shown_ref, k=k: (
                        shown_ref[k * survivor_count + d],
                        0,
                        0,
                        0,
                    ),
                )
                for k in range(group_count)
            ]
            + [pl.BlockSpec(memory_space=pl.ANY)] * (len(later) + len(before)),
            out_specs=[pl.BlockSpec((slab_count, 1, rows, points), lambda d, *_: (0, d, 0, 0))]
            + [pl.BlockSpec(memory_space=pl.ANY)] * len(later),
        ),
        out_shape=[jax.ShapeDtypeStruct((slab_count, survivor_count, rows, points), jnp.bfloat16)]
        + [jax.ShapeDtypeStruct(w.shape, w.dtype) for w in later],
        input_output_aliases={2 + group_count + i: 1 + i for i in range(len(later))},
        compiler_params=params(),
        cost_estimate=cost(0, 4 * survivor_count * slab_count * rows * points),
    )(offset, shown, *sources, *later, *before)


def spread(place, slot_source, source, member_here, group_count):
    slab_count, _, rows, points = source.shape

    def source_at(k, t, place_ref, slot_ref):
        return 0, slot_ref[lax.bitwise_xor(place_ref[0], k) * member_here + t], 0, 0

    def kernel(place_ref, slot_ref, source_ref, *out_refs):
        for k in range(group_count):

            @pl.when(pl.program_id(0) == k)
            def _(k=k):
                out_refs[k][0] = source_ref[:, 0]

    return pl.pallas_call(
        kernel,
        name="spread",
        grid_spec=pltpu.PrefetchScalarGridSpec(
            num_scalar_prefetch=2,
            grid=(group_count, member_here),
            in_specs=[pl.BlockSpec((slab_count, 1, rows, points), source_at)],
            out_specs=[
                pl.BlockSpec(
                    (1, slab_count, rows, points),
                    lambda k, t, *_, own=own: (
                        jnp.where(k == own, t, jnp.where(k < own, 0, member_here - 1)),
                        0,
                        0,
                        0,
                    ),
                )
                for own in range(group_count)
            ],
        ),
        out_shape=[
            jax.ShapeDtypeStruct((member_here, slab_count, rows, points), jnp.bfloat16)
        ]
        * group_count,
        compiler_params=params(),
        cost_estimate=cost(0, 4 * group_count * member_here * slab_count * rows * points),
    )(place, slot_source, source)


def synthesise(place, table, sources, shape, part, cut, earlier):
    group_count, rows, lon_count = table.shape
    member_here, _, fields, lats, _ = shape
    points = sources[0].shape[2]

    def kernel(place_ref, table_ref, *refs):
        group = place_ref[0]
        total = dot(refs[0][0], table_ref[group], TN)
        for s in range(1, group_count):
            total += dot(refs[s][0], table_ref[lax.bitwise_xor(group, s)], TN)
        out_ref = refs[-1]
        if cut[0] > 0:
            out_ref[0, 0, :, : cut[0], :] = refs[group_count][0, 0, :, : cut[0], :]
        out_ref[0, 0, :, cut[0] : cut[1], :] = total.astype(jnp.bfloat16).reshape(
            fields, cut[1] - cut[0], lon_count
        )

    given = [place, table, *sources]
    whole = pl.BlockSpec((1, 1, fields, lats, lon_count), lambda t: (t, part, 0, 0, 0))
    specs = [
        pl.BlockSpec(memory_space=pltpu.SMEM),
        pl.BlockSpec((group_count, rows, lon_count), lambda t: (0, 0, 0)),
    ] + [pl.BlockSpec((1, rows, points), lambda t: (t, 0, 0))] * group_count
    aliases = {}
    if earlier is not None:
        aliases = {len(given): 0}
        given.append(earlier)
        specs.append(whole if cut[0] > 0 else pl.BlockSpec(memory_space=pl.ANY))
    return pl.pallas_call(
        kernel,
        name="synthesise",
        grid=(member_here,),
        in_specs=specs,
        out_specs=whole,
        out_shape=jax.ShapeDtypeStruct(shape, jnp.bfloat16),
        input_output_aliases=aliases,
        compiler_params=params(),
        cost_estimate=cost(
            2 * member_here * group_count * rows * lon_count * points,
            2 * member_here * points * (lon_count + group_count * rows),
        ),
    )(*given)


def spectral_filter(
    place, legendre, quad_weight, rates, sources, survivor_count, cuts_in, cuts_out, before
):
    slab_count, rows, _ = sources[0].shape
    field_here = rates.shape[0]
    lat_here = cuts_in[-1][1]
    points = field_here * lat_here
    wave_here, _, degree_count, hemisphere = legendre.shape
    lat_count = 2 * hemisphere
    half_slabs = slab_count // 2
    row_here = 2 * wave_here
    used = 2 * survivor_count
    padded = -(-used // 16) * 16

    shuffle = np.zeros((wave_here, padded, survivor_count, wave_here, 2), np.float32)
    for m in range(wave_here):
        for d in range(survivor_count):
            for r in range(2):
                shuffle[m, 2 * d + r, d, m, r] = 1.0
    shuffle = shuffle.reshape(wave_here * padded, survivor_count * row_here)
    gather = jnp.asarray(shuffle.astype(jnp.bfloat16))
    scatter = jnp.asarray(shuffle.T.astype(jnp.bfloat16))
    mirror = jnp.asarray(np.eye(hemisphere, dtype=np.float32)[::-1].astype(jnp.bfloat16))

    def kernel(
        place_ref,
        gather_ref,
        scatter_ref,
        mirror_ref,
        weight_ref,
        rate_ref,
        table_ref,
        *refs,
    ):
        source_refs = refs[: len(cuts_in)]
        out_refs = refs[len(cuts_in) + len(before) :][: len(cuts_out)]
        held, north_rows, south_rows = refs[-3:]
        m = pl.program_id(0)
        group, slab = place_ref[0], place_ref[1]

        @pl.when(m == 0)
        def _():
            for s in range(slab_count):
                for (low, high), source_ref in zip(cuts_in, source_refs):
                    held[s, :, field_here * low : field_here * high] = dot(
                        gather_ref[...], source_ref[s]
                    ).astype(jnp.bfloat16)

        here = pl.ds(pl.multiple_of(m * padded, 16), padded)
        for side, rows_ref in ((0, north_rows), (half_slabs, south_rows)):
            for g in range(half_slabs):
                row = held[side + g, here, :]
                for low, high in cuts_in:
                    for f in range(field_here):
                        at = field_here * low + f * (high - low)
                        rows_ref[
                            f * padded : (f + 1) * padded, g * lat_here + low : g * lat_here + high
                        ] = row[:, at : at + high - low]
        north = north_rows[...].astype(jnp.float32)
        south = dot(south_rows[...], mirror_ref[...])
        weight = weight_ref[...]
        wave = (group * slab_count + slab) * wave_here + m
        degree_index = lax.broadcasted_iota(jnp.int32, (1, degree_count), 1)
        returned = []
        for p in range(2):
            both = (north + south) if p == 0 else (north - south)
            paired = (both * weight).astype(jnp.bfloat16)
            spectrum = dot(paired, table_ref[0, p], NT)
            degree = 2 * degree_index + (wave + p) % 2
            ratio = (degree * (degree + 1)).astype(jnp.float32) / float(lat_count * (lat_count - 1))
            damping = 1.0 / (1.0 + rate_ref[...] * (ratio * ratio))
            damping = jnp.where(degree >= wave, damping, 0.0)
            filtered = jnp.concatenate(
                [
                    (spectrum[f * padded : (f + 1) * padded] * damping[f : f + 1]).astype(jnp.bfloat16)
                    for f in range(field_here)
                ],
                axis=0,
            )
            returned.append(dot(filtered, table_ref[0, p]))
        north_rows[...] = (returned[0] + returned[1]).astype(jnp.bfloat16)
        south_rows[...] = dot(
            (returned[0] - returned[1]).astype(jnp.bfloat16), mirror_ref[...]
        ).astype(jnp.bfloat16)
        for side, rows_ref in ((0, north_rows), (half_slabs, south_rows)):
            for g in range(half_slabs):
                for low, high in cuts_out:
                    for f in range(field_here):
                        at = field_here * low + f * (high - low)
                        held[side + g, here, at : at + high - low] = rows_ref[
                            f * padded : (f + 1) * padded, g * lat_here + low : g * lat_here + high
                        ]

        @pl.when(m == wave_here - 1)
        def _():
            for s in range(slab_count):
                for (low, high), out_ref in zip(cuts_out, out_refs):
                    out_ref[s] = dot(
                        scatter_ref[...], held[s, :, field_here * low : field_here * high]
                    ).astype(jnp.bfloat16)

    def fixed(*dims):
        return pl.BlockSpec(dims, lambda m: (0,) * len(dims), pipeline_mode=pl.Buffered(1))

    return pl.pallas_call(
        kernel,
        name="spectral",
        grid=(wave_here,),
        in_specs=[
            pl.BlockSpec(memory_space=pltpu.SMEM),
            fixed(*gather.shape),
            fixed(*scatter.shape),
            fixed(hemisphere, hemisphere),
            fixed(1, hemisphere),
            fixed(field_here, 1),
            pl.BlockSpec((1, 2, degree_count, hemisphere), lambda m: (m, 0, 0, 0)),
        ]
        + [fixed(*source.shape) for source in sources]
        + [pl.BlockSpec(memory_space=pl.ANY)] * len(before),
        out_specs=[fixed(slab_count, rows, field_here * (high - low)) for low, high in cuts_out],
        out_shape=[
            jax.ShapeDtypeStruct((slab_count, rows, field_here * (high - low)), jnp.bfloat16)
            for low, high in cuts_out
        ],
        scratch_shapes=[
            pltpu.VMEM((slab_count, wave_here * padded, points), jnp.bfloat16),
            pltpu.VMEM((field_here * padded, hemisphere), jnp.bfloat16),
            pltpu.VMEM((field_here * padded, hemisphere), jnp.bfloat16),
        ],
        compiler_params=params(),
        cost_estimate=cost(
            20 * 10**9, 2 * wave_here * 2 * degree_count * hemisphere + 4 * slab_count * rows * points
        ),
    )(
        place,
        gather,
        scatter,
        mirror,
        quad_weight[None, :],
        rates[:, None],
        legendre,
        *sources,
        *before,
    )


def latitude_cuts(lat_here):
    if lat_here % 16 or lat_here < 48:
        return [(0, lat_here)], [(0, lat_here)]
    short = max(16, lat_here * 2 // 5 // 16 * 16)
    return (
        [(0, short), (short, lat_here)],
        [(0, lat_here - short), (lat_here - short, lat_here)],
    )


def run(
    survivor_count, state, forward, inverse, survivors, slot_source, legendre, quad_weight, diffusion
):
    group_count = lax.axis_size("traj")
    slab_count = lax.axis_size("grid")
    place = jnp.stack([lax.axis_index("traj"), lax.axis_index("grid")]).astype(jnp.int32)
    member_here, _, fields, lats, lon_count = state.shape
    row_here = lon_count // (group_count * slab_count)
    field_here = diffusion.shape[0] // FIELD_PARTS
    lat_here = fields * lats // field_here
    first_in, last_out = latitude_cuts(lat_here)
    uncut = [(0, lat_here)]
    cuts_in = [first_in] + [uncut] * (FIELD_PARTS - 1)
    cuts_out = [uncut] * (FIELD_PARTS - 1) + [last_out]
    last = FIELD_PARTS - 1

    def dft_cut(cut):
        return cut if fields == field_here else (0, lats)

    def filtered(part, kept, before):
        out = spectral_filter(
            place,
            legendre,
            quad_weight,
            diffusion[part * field_here : (part + 1) * field_here],
            kept,
            survivor_count,
            cuts_in[part],
            cuts_out[part],
            before,
        )
        return [w.reshape(slab_count, survivor_count, row_here, w.shape[2]) for w in out]

    pieces = [(part, cut) for part in range(FIELD_PARTS) for cut in cuts_in[part]]
    arrived = [[] for _ in range(FIELD_PARTS)]
    back = []
    made = analyse(place, forward, state, pieces[0][0], dft_cut(pieces[0][1]))
    for i, (part, cut) in enumerate(pieces):
        waves = exchange(made, "traj")
        if i + 1 < len(pieces):
            made = analyse(place, forward, state, pieces[i + 1][0], dft_cut(pieces[i + 1][1]))
            later = list(made[1:])
        else:
            made, later = [], []
        points = waves[0].shape[2]
        waves = [w.reshape(member_here, slab_count, row_here, points) for w in waves]
        before = [back[-1][0]] if back else []
        kept, *later = keep(place, survivors, waves, survivor_count, later, before)
        made = [*made[:1], *later]
        arrived[part].append(
            transpose(kept).reshape(slab_count, survivor_count * row_here, points)
        )
        if part > 0:
            back.append(filtered(part - 1, arrived[part - 1], [kept]))

    smoothed = None
    for part in range(FIELD_PARTS):
        if part == last:
            back.append(filtered(part, arrived[part], []))
        for cut, rows in zip(cuts_out[part], back[part]):
            slots = exchange(
                spread(place, slot_source, transpose(rows), member_here, group_count), "traj"
            )
            slots = [w.reshape(member_here, slab_count * row_here, w.shape[3]) for w in slots]
            smoothed = synthesise(place, inverse, slots, state.shape, part, dft_cut(cut), smoothed)
    return smoothed


def on_device(state, counts, slot_perm, legendre, quad_weight, diffusion):
    survivors, slot_source = survivor_lists(counts, slot_perm)
    group_count = lax.axis_size("traj")
    member_here, field_count, lat_here, lon_count = state.shape
    forward, inverse = trig_tables(lon_count)
    forward = jnp.asarray(forward).reshape(group_count, -1, lon_count)
    inverse = jnp.asarray(inverse).reshape(group_count, -1, lon_count)
    field_here = field_count // FIELD_PARTS
    split = (field_here, lat_here) if lat_here % 16 == 0 else (1, field_here * lat_here)
    parts = state.reshape(member_here, FIELD_PARTS, *split, lon_count)
    most = counts.shape[0] - MOST_COPIES + 1
    sizes = range(min(LEAST_ROWS, most), most + 1)
    branch = jnp.clip(jnp.sum(counts > 0).astype(jnp.int32) - sizes[0], 0, len(sizes) - 1)
    smoothed = lax.switch(
        branch,
        [functools.partial(run, size) for size in sizes],
        parts,
        forward,
        inverse,
        survivors,
        slot_source,
        legendre,
        quad_weight,
        diffusion,
    )
    return smoothed.reshape(member_here, field_count, lat_here, lon_count)


def solution(mesh):
    return jax.shard_map(
        on_device,
        mesh=mesh,
        in_specs=(
            P("traj", None, "grid", None),
            P(),
            P(),
            P(("traj", "grid"), None, None, None),
            P(),
            P(),
        ),
        out_specs=P("traj", None, "grid", None),
        check_vma=False,
    )
```

```python
import functools
import math

import jax
import jax.numpy as jnp
import numpy as np
from jax import lax
from jax.experimental import pallas as pl
from jax.experimental.pallas import tpu as pltpu
from jax.sharding import PartitionSpec as P

FIELD_PARTS = 3
MOST_COPIES = 4
LEAST_ROWS = 8
VMEM_BYTES = 60 * 2**20
NT = (((1,), (1,)), ((), ()))
TN = (((0,), (0,)), ((), ()))


def parent_slots(counts, slot_perm):
    member_count = counts.shape[0]
    position = jnp.arange(member_count, dtype=jnp.int32)
    copy_end = jnp.cumsum(counts)
    copy_parent = jnp.sum((copy_end[None, :] <= position[:, None]).astype(jnp.int32), axis=1)
    landing = (slot_perm[:, None] == position[None, :]).astype(jnp.int32)
    return jnp.sum(landing * copy_parent[:, None], axis=0)


def survivor_lists(counts, slot_perm):
    member_count = counts.shape[0]
    position = jnp.arange(member_count, dtype=jnp.int32)
    alive = counts > 0
    rank = jnp.sum((position[None, :] < position[:, None]) & alive[None, :], axis=1).astype(jnp.int32)
    hit = alive[None, :] & (rank[None, :] == position[:, None])
    survivors = jnp.sum(hit * position[None, :], axis=1).astype(jnp.int32)
    parents = parent_slots(counts, slot_perm)
    slot_source = jnp.sum((parents[:, None] == position[None, :]) * rank[None, :], axis=1)
    return survivors, slot_source.astype(jnp.int32)


def trig_tables(lon_count):
    wave_count = lon_count // 2
    turn = np.arange(wave_count)[:, None] * np.arange(lon_count)[None, :] % lon_count
    phase = (turn.astype(np.float32) * np.float32(2.0 * math.pi / lon_count)).astype(np.float64)
    pair = np.stack([np.cos(phase), -np.sin(phase)], axis=1).astype(np.float32)
    doubled = np.where(np.arange(wave_count) == 0, 1.0, 2.0).astype(np.float32)
    forward = (pair / np.float32(lon_count)).astype(jnp.bfloat16)
    inverse = (pair * doubled[:, None, None]).astype(jnp.bfloat16)
    return forward.reshape(2 * wave_count, lon_count), inverse.reshape(2 * wave_count, lon_count)


def exchange(pieces, axis):
    size = lax.axis_size(axis)
    out = [pieces[0]]
    for s in range(1, size):
        out.append(lax.ppermute(pieces[s], axis, [(i, i ^ s) for i in range(size)]))
    return out


def transpose(blocks):
    return lax.all_to_all(blocks, "grid", split_axis=0, concat_axis=0, tiled=True)


def transpose_all(blocks):
    flat = blocks.reshape(-1, *blocks.shape[2:])
    flat = lax.all_to_all(flat, ("traj", "grid"), split_axis=0, concat_axis=0, tiled=True)
    return flat.reshape(blocks.shape)


def params():
    return pltpu.CompilerParams(vmem_limit_bytes=VMEM_BYTES)


def cost(flops, bytes_accessed):
    return pl.CostEstimate(flops=flops, bytes_accessed=bytes_accessed, transcendentals=0)


def dot(a, b, dims=(((1,), (0,)), ((), ()))):
    return lax.dot_general(a, b, dims, preferred_element_type=jnp.float32)


def gate(later, sources):
    if not later:
        return later
    passed = pl.BlockSpec(memory_space=pl.ANY)
    return pl.pallas_call(
        lambda *refs: None,
        name="gate",
        in_specs=[passed] * (len(later) + len(sources)),
        out_specs=[passed] * len(later),
        out_shape=[jax.ShapeDtypeStruct(w.shape, w.dtype) for w in later],
        input_output_aliases={i: i for i in range(len(later))},
        cost_estimate=cost(0, 0),
    )(*later, *sources)


def analyse(place, table, state, part, cut, slab_count=None, before=()):
    group_count, rows, lon_count = table.shape
    member_here, _, fields, lats, _ = state.shape
    points = fields * (cut[1] - cut[0])

    def kernel(place_ref, table_ref, state_ref, *refs):
        out_refs = refs[len(before) :]
        group = place_ref[0]
        block = state_ref[0, 0, :, cut[0] : cut[1], :].reshape(points, lon_count)
        for s in range(group_count):
            if slab_count:
                waves = dot(table_ref[s], block, NT)
                out_refs[0][s, :, 0] = waves.reshape(slab_count, -1, points).astype(jnp.bfloat16)
                continue
            out_refs[s][0] = dot(table_ref[lax.bitwise_xor(group, s)], block, NT).astype(jnp.bfloat16)

    if slab_count:
        dims = (group_count, slab_count, member_here, rows // slab_count, points)
        out_specs = pl.BlockSpec((*dims[:2], 1, *dims[3:]), lambda t: (0, 0, t, 0, 0))
        out_shape = jax.ShapeDtypeStruct(dims, jnp.bfloat16)
    else:
        dims = (member_here, rows, points)
        out_specs = [pl.BlockSpec((1, *dims[1:]), lambda t: (t, 0, 0))] * group_count
        out_shape = [jax.ShapeDtypeStruct(dims, jnp.bfloat16)] * group_count
    return pl.pallas_call(
        kernel,
        name="analyse",
        grid=(member_here,),
        in_specs=[
            pl.BlockSpec(memory_space=pltpu.SMEM),
            pl.BlockSpec((group_count, rows, lon_count), lambda t: (0, 0, 0)),
            pl.BlockSpec((1, 1, fields, lats, lon_count), lambda t: (t, part, 0, 0, 0)),
        ]
        + [pl.BlockSpec(memory_space=pl.ANY)] * len(before),
        out_specs=out_specs,
        out_shape=out_shape,
        compiler_params=params(),
        cost_estimate=cost(
            2 * member_here * group_count * rows * lon_count * points,
            2 * member_here * points * (lon_count + group_count * rows),
        ),
    )(place, table, state, *before)


def keep(place, survivors, sources, survivor_count, before):
    group_count = len(sources)
    member_here, slab_count, rows, points = sources[0].shape
    survivors = survivors[:survivor_count]
    offset = survivors // member_here ^ place[0]
    step = jnp.arange(survivor_count, dtype=jnp.int32)
    seen = (offset[None, None, :] == jnp.arange(group_count, dtype=jnp.int32)[:, None, None]) & (
        step[None, None, :] <= step[None, :, None]
    )
    shown = jnp.max(jnp.where(seen, survivors % member_here, 0), axis=2).reshape(-1)

    def kernel(offset_ref, shown_ref, *refs):
        out_ref = refs[-1]
        chosen = offset_ref[pl.program_id(0)]
        for k in range(group_count):

            @pl.when(chosen == k)
            def _(k=k):
                out_ref[:, 0] = refs[k][0]

    return pl.pallas_call(
        kernel,
        name="keep",
        grid_spec=pltpu.PrefetchScalarGridSpec(
            num_scalar_prefetch=2,
            grid=(survivor_count,),
            in_specs=[
                pl.BlockSpec(
                    (1, slab_count, rows, points),
                    lambda d, offset_ref, shown_ref, k=k: (
                        shown_ref[k * survivor_count + d],
                        0,
                        0,
                        0,
                    ),
                )
                for k in range(group_count)
            ]
            + [pl.BlockSpec(memory_space=pl.ANY)] * len(before),
            out_specs=pl.BlockSpec((slab_count, 1, rows, points), lambda d, *_: (0, d, 0, 0)),
        ),
        out_shape=jax.ShapeDtypeStruct((slab_count, survivor_count, rows, points), jnp.bfloat16),
        compiler_params=params(),
        cost_estimate=cost(0, 4 * survivor_count * slab_count * rows * points),
    )(offset, shown, *sources, *before)


def pick(survivors, source, survivor_count):
    _, slab_count, member_here, rows, points = source.shape

    def kernel(group_ref, member_ref, source_ref, out_ref):
        out_ref[:, 0] = source_ref[0, :, 0]

    return pl.pallas_call(
        kernel,
        name="pick",
        grid_spec=pltpu.PrefetchScalarGridSpec(
            num_scalar_prefetch=2,
            grid=(survivor_count,),
            in_specs=[
                pl.BlockSpec(
                    (1, slab_count, 1, rows, points),
                    lambda d, group_ref, member_ref: (group_ref[d], 0, member_ref[d], 0, 0),
                )
            ],
            out_specs=pl.BlockSpec((slab_count, 1, rows, points), lambda d, *_: (0, d, 0, 0)),
        ),
        out_shape=jax.ShapeDtypeStruct((slab_count, survivor_count, rows, points), jnp.bfloat16),
        compiler_params=params(),
        cost_estimate=cost(0, 4 * survivor_count * slab_count * rows * points),
    )(survivors // member_here, survivors % member_here, source)


def expand(slot_source, source, member_here, group_count, before):
    slab_count, _, rows, points = source.shape

    def kernel(slot_ref, source_ref, *refs):
        refs[-1][0, :, 0] = source_ref[:, 0]

    return pl.pallas_call(
        kernel,
        name="expand",
        grid_spec=pltpu.PrefetchScalarGridSpec(
            num_scalar_prefetch=1,
            grid=(group_count, member_here),
            in_specs=[
                pl.BlockSpec(
                    (slab_count, 1, rows, points),
                    lambda k, t, slot_ref: (0, slot_ref[k * member_here + t], 0, 0),
                )
            ]
            + [pl.BlockSpec(memory_space=pl.ANY)] * len(before),
            out_specs=pl.BlockSpec(
                (1, slab_count, 1, rows, points), lambda k, t, *_: (k, 0, t, 0, 0)
            ),
        ),
        out_shape=jax.ShapeDtypeStruct(
            (group_count, slab_count, member_here, rows, points), jnp.bfloat16
        ),
        compiler_params=params(),
        cost_estimate=cost(0, 4 * group_count * member_here * slab_count * rows * points),
    )(slot_source, source, *before)


def spread(place, slot_source, source, member_here, group_count):
    slab_count, _, rows, points = source.shape

    def source_at(k, t, place_ref, slot_ref):
        return 0, slot_ref[lax.bitwise_xor(place_ref[0], k) * member_here + t], 0, 0

    def kernel(place_ref, slot_ref, source_ref, *out_refs):
        for k in range(group_count):

            @pl.when(pl.program_id(0) == k)
            def _(k=k):
                out_refs[k][0] = source_ref[:, 0]

    return pl.pallas_call(
        kernel,
        name="spread",
        grid_spec=pltpu.PrefetchScalarGridSpec(
            num_scalar_prefetch=2,
            grid=(group_count, member_here),
            in_specs=[pl.BlockSpec((slab_count, 1, rows, points), source_at)],
            out_specs=[
                pl.BlockSpec(
                    (1, slab_count, rows, points),
                    lambda k, t, *_, own=own: (
                        jnp.where(k == own, t, jnp.where(k < own, 0, member_here - 1)),
                        0,
                        0,
                        0,
                    ),
                )
                for own in range(group_count)
            ],
        ),
        out_shape=[
            jax.ShapeDtypeStruct((member_here, slab_count, rows, points), jnp.bfloat16)
        ]
        * group_count,
        compiler_params=params(),
        cost_estimate=cost(0, 4 * group_count * member_here * slab_count * rows * points),
    )(place, slot_source, source)


def synthesise(place, table, sources, shape, part, cut, earlier):
    group_count, rows, lon_count = table.shape
    member_here, _, fields, lats, _ = shape
    joint = not isinstance(sources, list)
    sources = [sources] if joint else sources
    points = sources[0].shape[-1]
    source_count = len(sources)

    def kernel(place_ref, table_ref, *refs):
        group = place_ref[0]
        total = 0.0
        for s in range(group_count):
            if joint:
                rows_ref = refs[-1]
                slab_count, row_here = sources[0].shape[1], sources[0].shape[3]
                for g in range(slab_count):
                    rows_ref[s, g * row_here : (g + 1) * row_here] = refs[0][s, g, 0]
                total += dot(rows_ref[s], table_ref[s], TN)
            else:
                total += dot(refs[s][0], table_ref[lax.bitwise_xor(group, s)], TN)
        out_ref = refs[-2] if joint else refs[-1]
        if cut[0] > 0:
            out_ref[0, 0, :, : cut[0], :] = refs[source_count][0, 0, :, : cut[0], :]
        out_ref[0, 0, :, cut[0] : cut[1], :] = total.astype(jnp.bfloat16).reshape(
            fields, cut[1] - cut[0], lon_count
        )

    given = [place, table, *sources]
    whole = pl.BlockSpec((1, 1, fields, lats, lon_count), lambda t: (t, part, 0, 0, 0))
    specs = [
        pl.BlockSpec(memory_space=pltpu.SMEM),
        pl.BlockSpec((group_count, rows, lon_count), lambda t: (0, 0, 0)),
    ]
    if joint:
        dims = sources[0].shape
        specs.append(pl.BlockSpec((*dims[:2], 1, *dims[3:]), lambda t: (0, 0, t, 0, 0)))
    else:
        specs += [pl.BlockSpec((1, rows, points), lambda t: (t, 0, 0))] * group_count
    aliases = {}
    if earlier is not None:
        aliases = {len(given): 0}
        given.append(earlier)
        specs.append(whole if cut[0] > 0 else pl.BlockSpec(memory_space=pl.ANY))
    return pl.pallas_call(
        kernel,
        name="synthesise",
        grid=(member_here,),
        in_specs=specs,
        out_specs=whole,
        out_shape=jax.ShapeDtypeStruct(shape, jnp.bfloat16),
        scratch_shapes=[pltpu.VMEM((group_count, rows, points), jnp.bfloat16)] if joint else [],
        input_output_aliases=aliases,
        compiler_params=params(),
        cost_estimate=cost(
            2 * member_here * group_count * rows * lon_count * points,
            2 * member_here * points * (lon_count + group_count * rows),
        ),
    )(*given)


def spectral_filter(
    place, legendre, quad_weight, rates, sources, survivor_count, cuts_in, cuts_out, before
):
    slab_count, rows, _ = sources[0].shape
    field_here = rates.shape[0]
    lat_here = cuts_in[-1][1]
    points = field_here * lat_here
    wave_here, _, degree_count, hemisphere = legendre.shape
    lat_count = 2 * hemisphere
    half_slabs = slab_count // 2
    row_here = 2 * wave_here
    used = 2 * survivor_count
    padded = -(-used // 16) * 16

    shuffle = np.zeros((wave_here, padded, survivor_count, wave_here, 2), np.float32)
    for m in range(wave_here):
        for d in range(survivor_count):
            for r in range(2):
                shuffle[m, 2 * d + r, d, m, r] = 1.0
    shuffle = shuffle.reshape(wave_here * padded, survivor_count * row_here)
    gather = jnp.asarray(shuffle.astype(jnp.bfloat16))
    scatter = jnp.asarray(shuffle.T.astype(jnp.bfloat16))
    mirror = jnp.asarray(np.eye(hemisphere, dtype=np.float32)[::-1].astype(jnp.bfloat16))

    def kernel(
        place_ref,
        gather_ref,
        scatter_ref,
        mirror_ref,
        weight_ref,
        rate_ref,
        table_ref,
        *refs,
    ):
        source_refs = refs[: len(cuts_in)]
        out_refs = refs[len(cuts_in) + len(before) :][: len(cuts_out)]
        held, north_rows, south_rows = refs[-3:]
        m = pl.program_id(0)
        group, slab = place_ref[0], place_ref[1]

        @pl.when(m == 0)
        def _():
            for s in range(slab_count):
                for (low, high), source_ref in zip(cuts_in, source_refs):
                    held[s, :, field_here * low : field_here * high] = dot(
                        gather_ref[...], source_ref[s]
                    ).astype(jnp.bfloat16)

        here = pl.ds(pl.multiple_of(m * padded, 16), padded)
        for side, rows_ref in ((0, north_rows), (half_slabs, south_rows)):
            for g in range(half_slabs):
                row = held[side + g, here, :]
                for low, high in cuts_in:
                    for f in range(field_here):
                        at = field_here * low + f * (high - low)
                        rows_ref[
                            f * padded : (f + 1) * padded, g * lat_here + low : g * lat_here + high
                        ] = row[:, at : at + high - low]
        north = north_rows[...].astype(jnp.float32)
        south = dot(south_rows[...], mirror_ref[...])
        weight = weight_ref[...]
        wave = (group * slab_count + slab) * wave_here + m
        degree_index = lax.broadcasted_iota(jnp.int32, (1, degree_count), 1)
        returned = []
        for p in range(2):
            both = (north + south) if p == 0 else (north - south)
            paired = (both * weight).astype(jnp.bfloat16)
            spectrum = dot(paired, table_ref[0, p], NT)
            degree = 2 * degree_index + (wave + p) % 2
            ratio = (degree * (degree + 1)).astype(jnp.float32) / float(lat_count * (lat_count - 1))
            damping = 1.0 / (1.0 + rate_ref[...] * (ratio * ratio))
            damping = jnp.where(degree >= wave, damping, 0.0)
            filtered = jnp.concatenate(
                [
                    (spectrum[f * padded : (f + 1) * padded] * damping[f : f + 1]).astype(jnp.bfloat16)
                    for f in range(field_here)
                ],
                axis=0,
            )
            returned.append(dot(filtered, table_ref[0, p]))
        north_rows[...] = (returned[0] + returned[1]).astype(jnp.bfloat16)
        south_rows[...] = dot(
            (returned[0] - returned[1]).astype(jnp.bfloat16), mirror_ref[...]
        ).astype(jnp.bfloat16)
        for side, rows_ref in ((0, north_rows), (half_slabs, south_rows)):
            for g in range(half_slabs):
                for low, high in cuts_out:
                    for f in range(field_here):
                        at = field_here * low + f * (high - low)
                        held[side + g, here, at : at + high - low] = rows_ref[
                            f * padded : (f + 1) * padded, g * lat_here + low : g * lat_here + high
                        ]

        @pl.when(m == wave_here - 1)
        def _():
            for s in range(slab_count):
                for (low, high), out_ref in zip(cuts_out, out_refs):
                    out_ref[s] = dot(
                        scatter_ref[...], held[s, :, field_here * low : field_here * high]
                    ).astype(jnp.bfloat16)

    def fixed(*dims):
        return pl.BlockSpec(dims, lambda m: (0,) * len(dims), pipeline_mode=pl.Buffered(1))

    return pl.pallas_call(
        kernel,
        name="spectral",
        grid=(wave_here,),
        in_specs=[
            pl.BlockSpec(memory_space=pltpu.SMEM),
            fixed(*gather.shape),
            fixed(*scatter.shape),
            fixed(hemisphere, hemisphere),
            fixed(1, hemisphere),
            fixed(field_here, 1),
            pl.BlockSpec((1, 2, degree_count, hemisphere), lambda m: (m, 0, 0, 0)),
        ]
        + [fixed(*source.shape) for source in sources]
        + [pl.BlockSpec(memory_space=pl.ANY)] * len(before),
        out_specs=[fixed(slab_count, rows, field_here * (high - low)) for low, high in cuts_out],
        out_shape=[
            jax.ShapeDtypeStruct((slab_count, rows, field_here * (high - low)), jnp.bfloat16)
            for low, high in cuts_out
        ],
        scratch_shapes=[
            pltpu.VMEM((slab_count, wave_here * padded, points), jnp.bfloat16),
            pltpu.VMEM((field_here * padded, hemisphere), jnp.bfloat16),
            pltpu.VMEM((field_here * padded, hemisphere), jnp.bfloat16),
        ],
        compiler_params=params(),
        cost_estimate=cost(
            20 * 10**9, 2 * wave_here * 2 * degree_count * hemisphere + 4 * slab_count * rows * points
        ),
    )(
        place,
        gather,
        scatter,
        mirror,
        quad_weight[None, :],
        rates[:, None],
        legendre,
        *sources,
        *before,
    )


def latitude_cuts(lat_here):
    if lat_here % 16 or lat_here < 48:
        return [(0, lat_here)], [(0, lat_here)]
    short = max(16, lat_here * 2 // 5 // 16 * 16)
    return (
        [(0, short), (short, lat_here)],
        [(0, lat_here - short), (lat_here - short, lat_here)],
    )


def run(
    survivor_count, state, forward, inverse, survivors, slot_source, legendre, quad_weight, diffusion
):
    group_count = lax.axis_size("traj")
    slab_count = lax.axis_size("grid")
    place = jnp.stack([lax.axis_index("traj"), lax.axis_index("grid")]).astype(jnp.int32)
    member_here, _, fields, lats, lon_count = state.shape
    row_here = lon_count // (group_count * slab_count)
    field_here = diffusion.shape[0] // FIELD_PARTS
    lat_here = fields * lats // field_here
    first_in, last_out = latitude_cuts(lat_here)
    uncut = [(0, lat_here)]
    cuts_in = [first_in] + [uncut] * (FIELD_PARTS - 1)
    cuts_out = [uncut] * (FIELD_PARTS - 1) + [last_out]
    last = FIELD_PARTS - 1

    def dft_cut(cut):
        return cut if fields == field_here else (0, lats)

    def filtered(part, kept, before):
        out = spectral_filter(
            place,
            legendre,
            quad_weight,
            diffusion[part * field_here : (part + 1) * field_here],
            kept,
            survivor_count,
            cuts_in[part],
            cuts_out[part],
            before,
        )
        return [w.reshape(slab_count, survivor_count, row_here, w.shape[2]) for w in out]

    pieces = [(part, cut) for part in range(FIELD_PARTS) for cut in cuts_in[part]]
    arrived = [[] for _ in range(FIELD_PARTS)]
    back, before = [], []
    if len(first_in) > 1:
        part, cut = pieces.pop(0)
        sent = analyse(place, forward, state, part, dft_cut(cut), slab_count)
        straight = pick(survivors, transpose_all(sent), survivor_count)
        arrived[part].append(straight.reshape(slab_count, survivor_count * row_here, -1))
        before = [sent]
    made = analyse(place, forward, state, pieces[0][0], dft_cut(pieces[0][1]), before=before)
    for i, (part, cut) in enumerate(pieces):
        waves = exchange(made, "traj")
        if i + 1 < len(pieces):
            made = analyse(place, forward, state, pieces[i + 1][0], dft_cut(pieces[i + 1][1]))
            made = [made[0], *gate(made[1:], waves[1:])]
        points = waves[0].shape[2]
        waves = [w.reshape(member_here, slab_count, row_here, points) for w in waves]
        before = [made[1]] if i + 1 < len(pieces) else []
        before += [back[-1][0]] if back else []
        kept = keep(place, survivors, waves, survivor_count, before)
        arrived[part].append(
            transpose(kept).reshape(slab_count, survivor_count * row_here, points)
        )
        if part > 0:
            back.append(filtered(part - 1, arrived[part - 1], [kept]))

    back.append(filtered(last, arrived[last], []))
    smoothed, slots = None, []
    for part in range(FIELD_PARTS):
        for cut, rows in zip(cuts_out[part], back[part]):
            if len(last_out) > 1 and part == last and cut == last_out[-1]:
                sent = expand(slot_source, rows, member_here, group_count, ready)
                slots = transpose_all(gate([sent], [crossed])[0])
            else:
                crossed = transpose(rows)
                sent = spread(place, slot_source, crossed, member_here, group_count)
                if part < last:
                    ready = [sent[1]]
                slots = exchange(sent, "traj")
                slots = [w.reshape(member_here, slab_count * row_here, -1) for w in slots]
            smoothed = synthesise(place, inverse, slots, state.shape, part, dft_cut(cut), smoothed)
    return smoothed


def on_device(state, counts, slot_perm, legendre, quad_weight, diffusion):
    survivors, slot_source = survivor_lists(counts, slot_perm)
    group_count = lax.axis_size("traj")
    member_here, field_count, lat_here, lon_count = state.shape
    forward, inverse = trig_tables(lon_count)
    forward = jnp.asarray(forward).reshape(group_count, -1, lon_count)
    inverse = jnp.asarray(inverse).reshape(group_count, -1, lon_count)
    field_here = field_count // FIELD_PARTS
    split = (field_here, lat_here) if lat_here % 16 == 0 else (1, field_here * lat_here)
    parts = state.reshape(member_here, FIELD_PARTS, *split, lon_count)
    most = counts.shape[0] - MOST_COPIES + 1
    sizes = range(min(LEAST_ROWS, most), most + 1)
    branch = jnp.clip(jnp.sum(counts > 0).astype(jnp.int32) - sizes[0], 0, len(sizes) - 1)
    smoothed = lax.switch(
        branch,
        [functools.partial(run, size) for size in sizes],
        parts,
        forward,
        inverse,
        survivors,
        slot_source,
        legendre,
        quad_weight,
        diffusion,
    )
    return smoothed.reshape(member_here, field_count, lat_here, lon_count)


def solution(mesh):
    return jax.shard_map(
        on_device,
        mesh=mesh,
        in_specs=(
            P("traj", None, "grid", None),
            P(),
            P(),
            P(("traj", "grid"), None, None, None),
            P(),
            P(),
        ),
        out_specs=P("traj", None, "grid", None),
        check_vma=False,
    )
```

```python
import functools
import math

import jax
import jax.numpy as jnp
import numpy as np
from jax import lax
from jax.experimental import pallas as pl
from jax.experimental.pallas import tpu as pltpu
from jax.sharding import PartitionSpec as P

FIELD_PARTS = 3
MOST_COPIES = 4
LEAST_ROWS = 8
BRANCH_ORDER = (2, 1, 4, 3, 0, 5)
TOKEN = (8, 128)
VMEM_BYTES = 60 * 2**20
NT = (((1,), (1,)), ((), ()))
TN = (((0,), (0,)), ((), ()))


def parent_slots(counts, slot_perm):
    member_count = counts.shape[0]
    position = jnp.arange(member_count, dtype=jnp.int32)
    copy_end = jnp.cumsum(counts)
    copy_parent = jnp.sum((copy_end[None, :] <= position[:, None]).astype(jnp.int32), axis=1)
    landing = (slot_perm[:, None] == position[None, :]).astype(jnp.int32)
    return jnp.sum(landing * copy_parent[:, None], axis=0)


def survivor_lists(counts, slot_perm):
    member_count = counts.shape[0]
    position = jnp.arange(member_count, dtype=jnp.int32)
    alive = counts > 0
    rank = jnp.sum((position[None, :] < position[:, None]) & alive[None, :], axis=1).astype(jnp.int32)
    hit = alive[None, :] & (rank[None, :] == position[:, None])
    survivors = jnp.sum(hit * position[None, :], axis=1).astype(jnp.int32)
    parents = parent_slots(counts, slot_perm)
    slot_source = jnp.sum((parents[:, None] == position[None, :]) * rank[None, :], axis=1)
    return survivors, slot_source.astype(jnp.int32)


def trig_tables(lon_count):
    wave_count = lon_count // 2
    turn = np.arange(wave_count)[:, None] * np.arange(lon_count)[None, :] % lon_count
    phase = (turn.astype(np.float32) * np.float32(2.0 * math.pi / lon_count)).astype(np.float64)
    pair = np.stack([np.cos(phase), -np.sin(phase)], axis=1).astype(np.float32)
    doubled = np.where(np.arange(wave_count) == 0, 1.0, 2.0).astype(np.float32)
    forward = (pair / np.float32(lon_count)).astype(jnp.bfloat16)
    inverse = (pair * doubled[:, None, None]).astype(jnp.bfloat16)
    return forward.reshape(2 * wave_count, lon_count), inverse.reshape(2 * wave_count, lon_count)


def exchange(pieces, axis):
    size = lax.axis_size(axis)
    out = [pieces[0]]
    for s in range(1, size):
        out.append(lax.ppermute(pieces[s], axis, [(i, i ^ s) for i in range(size)]))
    return out


def transpose(blocks):
    return lax.all_to_all(blocks, "grid", split_axis=0, concat_axis=0, tiled=True)


def params():
    return pltpu.CompilerParams(vmem_limit_bytes=VMEM_BYTES)


def cost(flops, bytes_accessed):
    return pl.CostEstimate(flops=flops, bytes_accessed=bytes_accessed, transcendentals=0)


def dot(a, b, dims=(((1,), (0,)), ((), ()))):
    return lax.dot_general(a, b, dims, preferred_element_type=jnp.float32)


def gate(later, sources):
    if not later:
        return later
    passed = pl.BlockSpec(memory_space=pl.ANY)
    return pl.pallas_call(
        lambda *refs: None,
        name="gate",
        in_specs=[passed] * (len(later) + len(sources)),
        out_specs=[passed] * len(later),
        out_shape=[jax.ShapeDtypeStruct(w.shape, w.dtype) for w in later],
        input_output_aliases={i: i for i in range(len(later))},
        cost_estimate=cost(0, 0),
    )(*later, *sources)


def analyse(place, table, state, part, cut):
    group_count, rows, lon_count = table.shape
    member_here, _, fields, lats, _ = state.shape
    points = fields * (cut[1] - cut[0])

    def kernel(place_ref, table_ref, state_ref, *out_refs):
        group = place_ref[0]
        block = state_ref[0, 0, :, cut[0] : cut[1], :].reshape(points, lon_count)
        for s in range(group_count):
            out_refs[s][0] = dot(table_ref[lax.bitwise_xor(group, s)], block, NT).astype(jnp.bfloat16)

    return pl.pallas_call(
        kernel,
        name="analyse",
        grid=(member_here,),
        in_specs=[
            pl.BlockSpec(memory_space=pltpu.SMEM),
            pl.BlockSpec((group_count, rows, lon_count), lambda t: (0, 0, 0)),
            pl.BlockSpec((1, 1, fields, lats, lon_count), lambda t: (t, part, 0, 0, 0)),
        ],
        out_specs=[pl.BlockSpec((1, rows, points), lambda t: (t, 0, 0))] * group_count,
        out_shape=[jax.ShapeDtypeStruct((member_here, rows, points), jnp.bfloat16)] * group_count,
        compiler_params=params(),
        cost_estimate=cost(
            2 * member_here * group_count * rows * lon_count * points,
            2 * member_here * points * (lon_count + group_count * rows),
        ),
    )(place, table, state)


def keep(place, survivors, sources, survivor_count, before):
    group_count = len(sources)
    member_here, slab_count, rows, points = sources[0].shape
    survivors = survivors[:survivor_count]
    offset = survivors // member_here ^ place[0]
    step = jnp.arange(survivor_count, dtype=jnp.int32)
    seen = (offset[None, None, :] == jnp.arange(group_count, dtype=jnp.int32)[:, None, None]) & (
        step[None, None, :] <= step[None, :, None]
    )
    shown = jnp.max(jnp.where(seen, survivors % member_here, 0), axis=2).reshape(-1)

    def kernel(offset_ref, shown_ref, *refs):
        out_ref = refs[-2]
        chosen = offset_ref[pl.program_id(0)]
        for k in range(group_count):

            @pl.when(chosen == k)
            def _(k=k):
                out_ref[:, 0] = refs[k][0]

    return pl.pallas_call(
        kernel,
        name="keep",
        grid_spec=pltpu.PrefetchScalarGridSpec(
            num_scalar_prefetch=2,
            grid=(survivor_count,),
            in_specs=[
                pl.BlockSpec(
                    (1, slab_count, rows, points),
                    lambda d, offset_ref, shown_ref, k=k: (
                        shown_ref[k * survivor_count + d],
                        0,
                        0,
                        0,
                    ),
                )
                for k in range(group_count)
            ]
            + [pl.BlockSpec(memory_space=pl.ANY)] * len(before),
            out_specs=[
                pl.BlockSpec((slab_count, 1, rows, points), lambda d, *_: (0, d, 0, 0)),
                pl.BlockSpec(memory_space=pl.ANY),
            ],
        ),
        out_shape=[
            jax.ShapeDtypeStruct((slab_count, survivor_count, rows, points), jnp.bfloat16),
            jax.ShapeDtypeStruct(TOKEN, jnp.float32),
        ],
        compiler_params=params(),
        cost_estimate=cost(0, 4 * survivor_count * slab_count * rows * points),
    )(offset, shown, *sources, *before)


def spread(place, slot_source, source, member_here, group_count):
    slab_count, _, rows, points = source.shape

    def source_at(k, t, place_ref, slot_ref):
        return 0, slot_ref[lax.bitwise_xor(place_ref[0], k) * member_here + t], 0, 0

    def kernel(place_ref, slot_ref, source_ref, *out_refs):
        for k in range(group_count):

            @pl.when(pl.program_id(0) == k)
            def _(k=k):
                out_refs[k][0] = source_ref[:, 0]

    return pl.pallas_call(
        kernel,
        name="spread",
        grid_spec=pltpu.PrefetchScalarGridSpec(
            num_scalar_prefetch=2,
            grid=(group_count, member_here),
            in_specs=[pl.BlockSpec((slab_count, 1, rows, points), source_at)],
            out_specs=[
                pl.BlockSpec(
                    (1, slab_count, rows, points),
                    lambda k, t, *_, own=own: (
                        jnp.where(k == own, t, jnp.where(k < own, 0, member_here - 1)),
                        0,
                        0,
                        0,
                    ),
                )
                for own in range(group_count)
            ],
        ),
        out_shape=[
            jax.ShapeDtypeStruct((member_here, slab_count, rows, points), jnp.bfloat16)
        ]
        * group_count,
        compiler_params=params(),
        cost_estimate=cost(0, 4 * group_count * member_here * slab_count * rows * points),
    )(place, slot_source, source)


def synthesise(place, table, sources, shape, part, cut, earlier):
    group_count, rows, lon_count = table.shape
    member_here, _, fields, lats, _ = shape
    points = sources[0].shape[2]

    def kernel(place_ref, table_ref, *refs):
        group = place_ref[0]
        total = dot(refs[0][0], table_ref[group], TN)
        for s in range(1, group_count):
            total += dot(refs[s][0], table_ref[lax.bitwise_xor(group, s)], TN)
        out_ref = refs[-1]
        if cut[0] > 0:
            out_ref[0, 0, :, : cut[0], :] = refs[group_count][0, 0, :, : cut[0], :]
        out_ref[0, 0, :, cut[0] : cut[1], :] = total.astype(jnp.bfloat16).reshape(
            fields, cut[1] - cut[0], lon_count
        )

    given = [place, table, *sources]
    whole = pl.BlockSpec((1, 1, fields, lats, lon_count), lambda t: (t, part, 0, 0, 0))
    specs = [
        pl.BlockSpec(memory_space=pltpu.SMEM),
        pl.BlockSpec((group_count, rows, lon_count), lambda t: (0, 0, 0)),
    ] + [pl.BlockSpec((1, rows, points), lambda t: (t, 0, 0))] * group_count
    aliases = {}
    if earlier is not None:
        aliases = {len(given): 0}
        given.append(earlier)
        specs.append(whole if cut[0] > 0 else pl.BlockSpec(memory_space=pl.ANY))
    return pl.pallas_call(
        kernel,
        name="synthesise",
        grid=(member_here,),
        in_specs=specs,
        out_specs=whole,
        out_shape=jax.ShapeDtypeStruct(shape, jnp.bfloat16),
        input_output_aliases=aliases,
        compiler_params=params(),
        cost_estimate=cost(
            2 * member_here * group_count * rows * lon_count * points,
            2 * member_here * points * (lon_count + group_count * rows),
        ),
    )(*given)


def spectral_filter(
    place, legendre, quad_weight, rates, sources, survivor_count, cuts_in, cuts_out, before
):
    slab_count, rows, _ = sources[0].shape
    field_here = rates.shape[0]
    lat_here = cuts_in[-1][1]
    points = field_here * lat_here
    wave_here, _, degree_count, hemisphere = legendre.shape
    lat_count = 2 * hemisphere
    half_slabs = slab_count // 2
    row_here = 2 * wave_here
    used = 2 * survivor_count
    padded = -(-used // 16) * 16

    shuffle = np.zeros((wave_here, padded, survivor_count, wave_here, 2), np.float32)
    for m in range(wave_here):
        for d in range(survivor_count):
            for r in range(2):
                shuffle[m, 2 * d + r, d, m, r] = 1.0
    shuffle = shuffle.reshape(wave_here * padded, survivor_count * row_here)
    gather = jnp.asarray(shuffle.astype(jnp.bfloat16))
    scatter = jnp.asarray(shuffle.T.astype(jnp.bfloat16))
    mirror = jnp.asarray(np.eye(hemisphere, dtype=np.float32)[::-1].astype(jnp.bfloat16))

    def kernel(
        place_ref,
        gather_ref,
        scatter_ref,
        mirror_ref,
        weight_ref,
        rate_ref,
        table_ref,
        *refs,
    ):
        source_refs = refs[: len(cuts_in)]
        out_refs = refs[len(cuts_in) + len(before) :][: len(cuts_out)]
        held, north_rows, south_rows = refs[-3:]
        m = pl.program_id(0)
        group, slab = place_ref[0], place_ref[1]

        @pl.when(m == 0)
        def _():
            for s in range(slab_count):
                for (low, high), source_ref in zip(cuts_in, source_refs):
                    held[s, :, field_here * low : field_here * high] = dot(
                        gather_ref[...], source_ref[s]
                    ).astype(jnp.bfloat16)

        here = pl.ds(pl.multiple_of(m * padded, 16), padded)
        for side, rows_ref in ((0, north_rows), (half_slabs, south_rows)):
            for g in range(half_slabs):
                row = held[side + g, here, :]
                for low, high in cuts_in:
                    for f in range(field_here):
                        at = field_here * low + f * (high - low)
                        rows_ref[
                            f * padded : (f + 1) * padded, g * lat_here + low : g * lat_here + high
                        ] = row[:, at : at + high - low]
        north = north_rows[...].astype(jnp.float32)
        south = dot(south_rows[...], mirror_ref[...])
        weight = weight_ref[...]
        wave = (group * slab_count + slab) * wave_here + m
        degree_index = lax.broadcasted_iota(jnp.int32, (1, degree_count), 1)
        returned = []
        for p in range(2):
            both = (north + south) if p == 0 else (north - south)
            paired = (both * weight).astype(jnp.bfloat16)
            spectrum = dot(paired, table_ref[0, p], NT)
            degree = 2 * degree_index + (wave + p) % 2
            ratio = (degree * (degree + 1)).astype(jnp.float32) / float(lat_count * (lat_count - 1))
            damping = 1.0 / (1.0 + rate_ref[...] * (ratio * ratio))
            damping = jnp.where(degree >= wave, damping, 0.0)
            filtered = jnp.concatenate(
                [
                    (spectrum[f * padded : (f + 1) * padded] * damping[f : f + 1]).astype(jnp.bfloat16)
                    for f in range(field_here)
                ],
                axis=0,
            )
            returned.append(dot(filtered, table_ref[0, p]))
        north_rows[...] = (returned[0] + returned[1]).astype(jnp.bfloat16)
        south_rows[...] = dot(
            (returned[0] - returned[1]).astype(jnp.bfloat16), mirror_ref[...]
        ).astype(jnp.bfloat16)
        for side, rows_ref in ((0, north_rows), (half_slabs, south_rows)):
            for g in range(half_slabs):
                for low, high in cuts_out:
                    for f in range(field_here):
                        at = field_here * low + f * (high - low)
                        held[side + g, here, at : at + high - low] = rows_ref[
                            f * padded : (f + 1) * padded, g * lat_here + low : g * lat_here + high
                        ]

        @pl.when(m == wave_here - 1)
        def _():
            for s in range(slab_count):
                for (low, high), out_ref in zip(cuts_out, out_refs):
                    out_ref[s] = dot(
                        scatter_ref[...], held[s, :, field_here * low : field_here * high]
                    ).astype(jnp.bfloat16)

    def fixed(*dims):
        return pl.BlockSpec(dims, lambda m: (0,) * len(dims), pipeline_mode=pl.Buffered(1))

    return pl.pallas_call(
        kernel,
        name="spectral",
        grid=(wave_here,),
        in_specs=[
            pl.BlockSpec(memory_space=pltpu.SMEM),
            fixed(*gather.shape),
            fixed(*scatter.shape),
            fixed(hemisphere, hemisphere),
            fixed(1, hemisphere),
            fixed(field_here, 1),
            pl.BlockSpec((1, 2, degree_count, hemisphere), lambda m: (m, 0, 0, 0)),
        ]
        + [fixed(*source.shape) for source in sources]
        + [pl.BlockSpec(memory_space=pl.ANY)] * len(before),
        out_specs=[fixed(slab_count, rows, field_here * (high - low)) for low, high in cuts_out]
        + [pl.BlockSpec(memory_space=pl.ANY)],
        out_shape=[
            jax.ShapeDtypeStruct((slab_count, rows, field_here * (high - low)), jnp.bfloat16)
            for low, high in cuts_out
        ]
        + [jax.ShapeDtypeStruct(TOKEN, jnp.float32)],
        scratch_shapes=[
            pltpu.VMEM((slab_count, wave_here * padded, points), jnp.bfloat16),
            pltpu.VMEM((field_here * padded, hemisphere), jnp.bfloat16),
            pltpu.VMEM((field_here * padded, hemisphere), jnp.bfloat16),
        ],
        compiler_params=params(),
        cost_estimate=cost(
            20 * 10**9, 2 * wave_here * 2 * degree_count * hemisphere + 4 * slab_count * rows * points
        ),
    )(
        place,
        gather,
        scatter,
        mirror,
        quad_weight[None, :],
        rates[:, None],
        legendre,
        *sources,
        *before,
    )


def latitude_cuts(lat_here):
    if lat_here % 16 or lat_here < 48:
        return [(0, lat_here)], [(0, lat_here)]
    short = max(16, lat_here * 2 // 5 // 16 * 16)
    return (
        [(0, short), (short, lat_here)],
        [(0, lat_here - short), (lat_here - short, lat_here)],
    )


def run(
    survivor_count, state, forward, inverse, survivors, slot_source, legendre, quad_weight, diffusion
):
    group_count = lax.axis_size("traj")
    slab_count = lax.axis_size("grid")
    place = jnp.stack([lax.axis_index("traj"), lax.axis_index("grid")]).astype(jnp.int32)
    member_here, _, fields, lats, lon_count = state.shape
    row_here = lon_count // (group_count * slab_count)
    field_here = diffusion.shape[0] // FIELD_PARTS
    lat_here = fields * lats // field_here
    first_in, last_out = latitude_cuts(lat_here)
    uncut = [(0, lat_here)]
    cuts_in = [first_in] + [uncut] * (FIELD_PARTS - 1)
    cuts_out = [uncut] + [last_out] * (FIELD_PARTS - 1)
    last = FIELD_PARTS - 1

    def dft_cut(cut):
        return cut if fields == field_here else (0, lats)

    def filtered(part, kept, before):
        *out, token = spectral_filter(
            place,
            legendre,
            quad_weight,
            diffusion[part * field_here : (part + 1) * field_here],
            kept,
            survivor_count,
            cuts_in[part],
            cuts_out[part],
            before,
        )
        return [w.reshape(slab_count, survivor_count, row_here, w.shape[2]) for w in out], token

    crossed, landed = [], {}

    def cross(rows):
        if crossed:
            after = landed.get(len(crossed) - 2, [])
            rows = gate([rows], [crossed[-1], *after])[0]
        crossed.append(transpose(rows))
        return crossed[-1]

    def go_back(part):
        nonlocal smoothed, went
        for cut, rows in zip(cuts_out[part], back[part]):
            came = cross(rows)
            sent = spread(place, slot_source, came, member_here, group_count)
            went = [sent[1]]
            slots = exchange(sent, "traj")
            landed[len(crossed) - 1] = slots[1:]
            slots = [w.reshape(member_here, slab_count * row_here, -1) for w in slots]
            smoothed = synthesise(place, inverse, slots, state.shape, part, dft_cut(cut), smoothed)

    pieces = [(part, cut) for part in range(FIELD_PARTS) for cut in cuts_in[part]]
    arrived = [[] for _ in range(FIELD_PARTS)]
    back, went, tokens, smoothed = [], [], [], None
    made = analyse(place, forward, state, pieces[0][0], dft_cut(pieces[0][1]))
    for i, (part, cut) in enumerate(pieces):
        waves = exchange(made, "traj")
        before = tokens[-1:]
        if i + 1 < len(pieces):
            made = analyse(place, forward, state, pieces[i + 1][0], dft_cut(pieces[i + 1][1]))
            made = [made[0], *gate(made[1:], waves[1:])]
            before.append(made[1])
        points = waves[0].shape[2]
        waves = [w.reshape(member_here, slab_count, row_here, points) for w in waves]
        kept, token = keep(place, survivors, waves, survivor_count, before)
        arrived[part].append(
            cross(kept).reshape(slab_count, survivor_count * row_here, points)
        )
        if cut == cuts_in[part][-1] and part > 0:
            rows, filter_token = filtered(part - 1, arrived[part - 1], [token, *went])
            back.append(rows)
            tokens.append(filter_token)
            if part < last:
                go_back(part - 1)
    back.append(filtered(last, arrived[last], [])[0])
    for part in range(last - 1, FIELD_PARTS):
        go_back(part)
    return smoothed


def on_device(state, counts, slot_perm, legendre, quad_weight, diffusion):
    survivors, slot_source = survivor_lists(counts, slot_perm)
    group_count = lax.axis_size("traj")
    member_here, field_count, lat_here, lon_count = state.shape
    forward, inverse = trig_tables(lon_count)
    forward = jnp.asarray(forward).reshape(group_count, -1, lon_count)
    inverse = jnp.asarray(inverse).reshape(group_count, -1, lon_count)
    field_here = field_count // FIELD_PARTS
    split = (field_here, lat_here) if lat_here % 16 == 0 else (1, field_here * lat_here)
    parts = state.reshape(member_here, FIELD_PARTS, *split, lon_count)
    most = counts.shape[0] - MOST_COPIES + 1
    sizes = list(range(min(LEAST_ROWS, most), most + 1))
    if len(sizes) == len(BRANCH_ORDER):
        sizes = [sizes[i] for i in BRANCH_ORDER]
    distinct = jnp.clip(jnp.sum(counts > 0).astype(jnp.int32), min(sizes), max(sizes))
    branch = sum((distinct == size).astype(jnp.int32) * i for i, size in enumerate(sizes))
    smoothed = lax.switch(
        branch,
        [functools.partial(run, size) for size in sizes],
        parts,
        forward,
        inverse,
        survivors,
        slot_source,
        legendre,
        quad_weight,
        diffusion,
    )
    return smoothed.reshape(member_here, field_count, lat_here, lon_count)


def solution(mesh):
    return jax.shard_map(
        on_device,
        mesh=mesh,
        in_specs=(
            P("traj", None, "grid", None),
            P(),
            P(),
            P(("traj", "grid"), None, None, None),
            P(),
            P(),
        ),
        out_specs=P("traj", None, "grid", None),
        check_vma=False,
    )
```
